32 devices in a mesh: dp: 8 (over y, x, core), ctx: 4 (over z).
Axes of the slice: x: 2, y: 2, z: 4, core: 2. Of those that a mesh axis runs over, the one named last changes fastest.
Arguments:
- frames_in: bfloat16 [8, 256, 768], P('dp', 'ctx'), may hold values from -6 to 6
- segment_ids: int32 [8, 256], P('dp'), may hold values from 0 to 4, as said below
- span_ids: int32 [8, 256], P('dp'), may hold values from 0 to 3, as said below
- ffn_gain: float32 [768], replicated, may hold values from 0.1 to 1.9
- w_up: bfloat16 [768, 3072], P('dp', 'ctx'), may hold values from -0.21875 to 0.21875
- w_down: bfloat16 [768, 3072], P('dp', 'ctx'), may hold values from -0.109375 to 0.109375
- attn_gain: float32 [768], replicated, may hold values from 0.1 to 1.9
- w_query: bfloat16 [768, 2048], P('dp', 'ctx'), may hold values from -0.21875 to 0.21875
- w_key: bfloat16 [768, 2048], P('dp', 'ctx'), may hold values from -0.21875 to 0.21875
- w_value: bfloat16 [768, 2048], P('dp', 'ctx'), may hold values from -0.21875 to 0.21875
- w_out: bfloat16 [768, 2048], P('dp', 'ctx'), may hold values from -0.125 to 0.125
- offset_bias: float32 [16, 9], P('ctx'), may hold values from -2 to 257
- cotangent: bfloat16 [8, 256, 768], P('dp', 'ctx'), may hold values from -6 to 6
Outputs:
- block_out: bfloat16 [8, 256, 768], P('dp', 'ctx')
- grad_up: float32 [768, 3072], P('dp', 'ctx')
- grad_down: float32 [768, 3072], P('dp', 'ctx')
- grad_query: float32 [768, 2048], P('dp', 'ctx')
- grad_key: float32 [768, 2048], P('dp', 'ctx')
- grad_value: float32 [768, 2048], P('dp', 'ctx')
- grad_out: float32 [768, 2048], P('dp', 'ctx')
The draws below stay inside these ranges and needn't reach their ends.
Inputs may be any that keep to these rules, and one draw needn't show every extreme that they name: `segment_ids`: in each stream the utterance number starts at 0 and never falls; every utterance but the stream's last has 56 to 224 frames. `span_ids`: A frame's span number is its position within its utterance divided by 64, rounded down.
All inputs are finite; a program needn't handle non-finite values.
Results may differ from the reference program's by a relative error of at most 0.024.
Values may be sent and summed in bfloat16 or wider, within the bound.
No kernel may reach another device: no remote copies, remote signals or barrier semaphores. Data moves between devices by JAX's collectives and lax.ppermute only.
A program may use at most 128 MiB of HBM per device.

```python
import math
import jax
import jax.numpy as jnp
from jax import lax

D = 768
HEADS = 16
HEAD_DIM = 128
FF = 3072
SPAN = 64
LEFT = 8
INNER = 2048
FRAMES = 256
GROUPS = 8
MAXLEN = 224
MINLEN = 56
UTTS = 5
N_CTX = 4


def utterances(key):
    key = jax.random.fold_in(key, 11)
    lengths = jax.random.randint(key, (GROUPS, UTTS), MINLEN, MAXLEN + 1)
    first_slot = (jnp.arange(GROUPS)[:, None] == 0) & (jnp.arange(UTTS)[None, :] == 0)
    lengths = jnp.where(first_slot, MAXLEN, lengths)
    last_group = (jnp.arange(GROUPS)[:, None] == GROUPS - 1) & (jnp.arange(UTTS)[None, :] >= 0)
    lengths = jnp.where(last_group, MINLEN, lengths)
    ends = jnp.cumsum(lengths, axis=1)
    position = jnp.arange(FRAMES)
    passed = ends[:, None, :] <= position[None, :, None]
    segments = jnp.sum(passed.astype(jnp.int32), axis=2)
    starts = jnp.max(jnp.where(passed, ends[:, None, :], 0), axis=2)
    spans = (position[None, :] - starts) // SPAN
    return (segments.astype(jnp.int32), spans.astype(jnp.int32))


def draw_segment_ids(key, part):
    return utterances(key)[0]


def draw_span_ids(key, part):
    return utterances(key)[1]


def draw_offset_bias(key, part):
    key = jax.random.fold_in(key, 5)
    base_key = jax.random.fold_in(key, 0)
    base = jax.random.uniform(base_key, (HEADS, LEFT + 1), jnp.float32, -2.0, 2.0)
    return base


def shard_levels(stream_key, shape, pieces, low, largest):
    loudness, own = 1.0, jax.random.fold_in(stream_key, 6)
    for dim, parts in pieces:
        draws = jnp.exp(jax.random.uniform(jax.random.fold_in(own, dim), (parts,), jnp.float32, low / len(pieces), largest / len(pieces)))
        loudness = loudness * jnp.repeat(draws, shape[dim] // parts).reshape([-1 if axis == dim else 1 for axis in range(len(shape))])
    return loudness


def normal_values(key, dims, spread, limit, cuts=(), dtype=jnp.bfloat16):
    loudness = shard_levels(key, dims, cuts, -0.22, 0.18) if cuts else 1.0
    result = jax.random.normal(key, dims, jnp.float32) * spread * loudness
    return jnp.minimum(jnp.maximum(result, -limit), limit).astype(dtype)


def setup_inputs(seed: int = 0) -> dict:
    key_of = jax.random.split(jax.random.key(seed), 14)
    return {
        "frames_in": normal_values(key_of[0], (GROUPS, FRAMES, D), 1.0, 6.0, ((0, 8), (1, 4))),
        "segment_ids": draw_segment_ids(jax.random.fold_in(key_of[13], 71), 0),
        "span_ids": draw_span_ids(jax.random.fold_in(key_of[13], 71), 0),
        "ffn_gain": jnp.clip(1.0 + 0.18 * jax.random.normal(key_of[3], (D,), jnp.float32), 0.1, 1.9),
        "w_up": normal_values(key_of[4], (D, FF), D ** -0.5, 0.21875, ((0, 8), (1, 4))),
        "w_down": normal_values(key_of[5], (D, FF), FF ** -0.5, 0.109375, ((0, 8), (1, 4))),
        "attn_gain": jnp.clip(1.0 + 0.18 * jax.random.normal(key_of[6], (D,), jnp.float32), 0.1, 1.9),
        "w_query": normal_values(key_of[7], (D, INNER), D ** -0.5, 0.21875, ((0, 8), (1, 4))),
        "w_key": normal_values(key_of[8], (D, INNER), D ** -0.5, 0.21875, ((0, 8), (1, 4))),
        "w_value": normal_values(key_of[9], (D, INNER), D ** -0.5, 0.21875, ((0, 8), (1, 4))),
        "w_out": normal_values(key_of[10], (D, INNER), INNER ** -0.5, 0.125, ((0, 8), (1, 4))),
        "offset_bias": draw_offset_bias(jax.random.fold_in(key_of[13], 71), 0),
        "cotangent": normal_values(key_of[12], (GROUPS, FRAMES, D), 1.0, 6.0, ((0, 8), (1, 4))),
    }


def round_trip(values):
    return lax.optimization_barrier(values.astype(jnp.bfloat16)).astype(jnp.float32)

def layer_norm(values, gain):
    center = values - lax.optimization_barrier(jnp.mean(values, axis=-1, keepdims=True))
    variance = lax.optimization_barrier(jnp.mean(center * center, axis=-1, keepdims=True))
    return center * lax.rsqrt(variance + 1e-05) * gain

def norm_slope(values, upstream, gain):
    center = values - lax.optimization_barrier(jnp.mean(values, axis=-1, keepdims=True))
    variance = lax.optimization_barrier(jnp.mean(center * center, axis=-1, keepdims=True))
    inverse = lax.rsqrt(variance + 1e-05)
    normed = center * inverse
    scaled = upstream * gain
    first_mean = lax.optimization_barrier(jnp.mean(scaled, axis=-1, keepdims=True))
    second_mean = lax.optimization_barrier(jnp.mean(scaled * normed, axis=-1, keepdims=True))
    return inverse * (scaled - first_mean - normed * second_mean)

def silu_slope(pre):
    sigma = jax.nn.sigmoid(pre)
    return sigma * (1.0 + pre * (1.0 - sigma))

def span_bias(offset_bias, segments, spans):
    same_utt = segments[:, None] == segments[None, :]
    distance = spans[:, None] - spans[None, :]
    window = offset_bias.shape[1] - 1
    allowed = same_utt & (distance >= 0) & (distance <= window)
    bias = jnp.zeros((offset_bias.shape[0],) + distance.shape, jnp.float32)
    for offset_step in range(window + 1):
        bias = bias + jnp.where(distance[None] == offset_step, offset_bias[:, offset_step][:, None, None], 0.0)
    return (allowed, bias)

def block_terms(left, right, count):
    left_blocks = left.astype(jnp.float32).reshape(left.shape[0], count, -1)
    right_blocks = right.astype(jnp.float32).reshape(right.shape[0], count, -1)
    return jnp.einsum('fcj,dcj->cfd', left_blocks, right_blocks)

def reference(frames_in, segment_ids, span_ids, ffn_gain, w_up, w_down, attn_gain, w_query, w_key, w_value, w_out, offset_bias, cotangent):
    score_scale = HEAD_DIM ** (-0.5)
    cot_scale = 1.0 / math.sqrt(GROUPS * FRAMES)

    def one_group(totals, group):
        inputs, segments, spans, cot = group
        ffn_normed = layer_norm(inputs.astype(jnp.float32), ffn_gain).astype(jnp.bfloat16)
        ffn_pre = jnp.dot(ffn_normed, w_up, preferred_element_type=jnp.float32)
        ffn_hidden = jax.nn.silu(ffn_pre).astype(jnp.bfloat16)
        ffn_sum = lax.optimization_barrier(jnp.sum(round_trip(block_terms(ffn_hidden, w_down, N_CTX)), axis=0))
        mid = inputs.astype(jnp.float32) + 0.5 * ffn_sum
        attn_normed = layer_norm(mid, attn_gain).astype(jnp.bfloat16)

        def project(weight):
            made = jnp.dot(attn_normed, weight, preferred_element_type=jnp.float32)
            return made.astype(jnp.bfloat16).reshape(FRAMES, HEADS, HEAD_DIM)
        query_rows = project(w_query)
        key_rows = project(w_key)
        value_rows = project(w_value)
        allowed, bias = span_bias(offset_bias, segments, spans)
        scores = jnp.einsum('qhd,khd->hqk', query_rows.astype(jnp.float32), key_rows.astype(jnp.float32)) * score_scale + bias
        scores = jnp.where(allowed[None], scores, -1e+30)
        top_score = lax.optimization_barrier(jnp.max(scores, axis=-1, keepdims=True))
        expo = jnp.exp(scores - top_score)
        soft_weights = expo / lax.optimization_barrier(jnp.sum(expo, axis=-1, keepdims=True))
        soft_low = soft_weights.astype(jnp.bfloat16)
        context = jnp.einsum('hqk,khd->qhd', soft_low.astype(jnp.float32), value_rows.astype(jnp.float32))
        context = context.astype(jnp.bfloat16).reshape(FRAMES, INNER)
        attn_sum = lax.optimization_barrier(jnp.sum(round_trip(block_terms(context, w_out, N_CTX)), axis=0))
        out_rows = (mid + attn_sum).astype(jnp.bfloat16)
        scaled_cot = (cot.astype(jnp.float32) * cot_scale).astype(jnp.bfloat16)
        grad_out = jnp.dot(scaled_cot.T, context, preferred_element_type=jnp.float32)
        grad_context = jnp.dot(scaled_cot, w_out, preferred_element_type=jnp.float32)
        grad_context = grad_context.astype(jnp.bfloat16).reshape(FRAMES, HEADS, HEAD_DIM)
        grad_probs = jnp.einsum('qhd,khd->hqk', grad_context.astype(jnp.float32), value_rows.astype(jnp.float32))
        row_total = lax.optimization_barrier(jnp.sum(soft_weights * grad_probs, axis=-1, keepdims=True))
        grad_scores = (soft_weights * (grad_probs - row_total)).astype(jnp.bfloat16)
        grad_q_rows = jnp.einsum('hqk,khd->qhd', grad_scores.astype(jnp.float32), key_rows.astype(jnp.float32)) * score_scale
        grad_q_rows = grad_q_rows.astype(jnp.bfloat16).reshape(FRAMES, INNER)
        grad_k_rows = jnp.einsum('hqk,qhd->khd', grad_scores.astype(jnp.float32), query_rows.astype(jnp.float32)) * score_scale
        grad_k_rows = grad_k_rows.astype(jnp.bfloat16).reshape(FRAMES, INNER)
        grad_v_rows = jnp.einsum('hqk,qhd->khd', soft_low.astype(jnp.float32), grad_context.astype(jnp.float32))
        grad_v_rows = grad_v_rows.astype(jnp.bfloat16).reshape(FRAMES, INNER)
        grad_query = jnp.dot(attn_normed.T, grad_q_rows, preferred_element_type=jnp.float32)
        grad_key = jnp.dot(attn_normed.T, grad_k_rows, preferred_element_type=jnp.float32)
        grad_value = jnp.dot(attn_normed.T, grad_v_rows, preferred_element_type=jnp.float32)
        normed_terms = block_terms(grad_q_rows, w_query, N_CTX) + block_terms(grad_k_rows, w_key, N_CTX) + block_terms(grad_v_rows, w_value, N_CTX)
        grad_normed = lax.optimization_barrier(jnp.sum(round_trip(normed_terms), axis=0))
        grad_mid = (scaled_cot.astype(jnp.float32) + norm_slope(mid, grad_normed, attn_gain)).astype(jnp.bfloat16)
        grad_down = 0.5 * jnp.dot(grad_mid.T, ffn_hidden, preferred_element_type=jnp.float32)
        grad_hidden = 0.5 * jnp.dot(grad_mid, w_down, preferred_element_type=jnp.float32) * silu_slope(ffn_pre)
        grad_hidden = grad_hidden.astype(jnp.bfloat16)
        grad_up = jnp.dot(ffn_normed.T, grad_hidden, preferred_element_type=jnp.float32)
        terms = (grad_up, grad_down, grad_query, grad_key, grad_value, grad_out)
        totals = tuple((total + round_trip(term) for total, term in zip(totals, terms)))
        return (totals, out_rows)
    shapes = ((D, FF), (D, FF), (D, INNER), (D, INNER), (D, INNER), (D, INNER))
    start_totals = tuple((jnp.zeros(shape, jnp.float32) for shape in shapes))
    totals, block_out = lax.scan(one_group, start_totals, (frames_in, segment_ids, span_ids, cotangent))
    return (block_out, totals[0], totals[1], totals[2], totals[3], totals[4], totals[5])
```

```python
import functools
import math

import jax
import jax.numpy as jnp
from jax import lax
from jax.experimental import pallas as pl
from jax.experimental.pallas import tpu as pltpu
from jax.sharding import PartitionSpec as P

SPAN = 64
BF = jnp.bfloat16
F32 = jnp.float32
VMEM_BYTES = 56 * 1024 * 1024


def exchange(values, axis, mask):
    size = lax.axis_size(axis)
    return lax.ppermute(values, axis, [(one, one ^ mask) for one in range(size)])


def call(body, outs, args, scratch=(), flops=0, smem=0):
    specs = [pl.BlockSpec(memory_space=pltpu.SMEM)] * smem
    specs += [pl.BlockSpec(memory_space=pltpu.VMEM)] * (len(args) - smem)
    moved = sum(math.prod(one.shape) * one.dtype.itemsize for one in list(args) + list(outs))
    return pl.pallas_call(
        body,
        out_shape=tuple(outs),
        in_specs=specs,
        out_specs=tuple(pl.BlockSpec(memory_space=pltpu.VMEM) for _ in outs),
        scratch_shapes=list(scratch),
        compiler_params=pltpu.CompilerParams(vmem_limit_bytes=VMEM_BYTES),
        cost_estimate=pl.CostEstimate(flops=flops, bytes_accessed=moved, transcendentals=0),
    )(*args)


def shape(dims, dtype):
    return jax.ShapeDtypeStruct(dims, dtype)


def dot(left, right, left_dim, right_dim):
    return lax.dot_general(
        left, right, (((left_dim,), (right_dim,)), ((), ())), preferred_element_type=F32
    )


def normalise(values):
    center = values - jnp.mean(values, axis=-1, keepdims=True)
    variance = jnp.mean(center * center, axis=-1, keepdims=True)
    inverse = lax.rsqrt(variance + 1e-05)
    return center * inverse, inverse


def collect(me_ref, pieces, ids, target, columns=None):
    rows = pieces[0].shape[0]
    for piece, mask in zip(pieces, ids):
        if len(ids) == 1:
            first = 0
        else:
            first = pl.multiple_of((me_ref[0] ^ mask) * rows, 16)
        target[pl.ds(first, rows), :] = piece[...]


def hand_out(me_ref, total, ids, outs, first_column):
    width = total.shape[1]
    rows = outs[0].shape[0]
    for out, mask in zip(outs, ids):
        if len(ids) == 1:
            first = 0
        else:
            first = pl.multiple_of((me_ref[0] ^ mask) * rows, 8)
        out[:, first_column : first_column + width] = total[pl.ds(first, rows), :].astype(BF)


def ffn_kernel(parts, ids, *refs):
    count = len(ids)
    me_ref, gain = refs[0], refs[1]
    frames = refs[2 : 2 + parts]
    ups = refs[2 + parts : 2 + parts + count]
    downs = refs[2 + parts + count : 2 + parts + 2 * count]
    rest = refs[2 + parts + 2 * count :]
    normed_out, pre_out, hidden_out = rest[:3]
    partials = rest[3 : 3 + parts]
    up, down = rest[3 + parts :]
    collect(me_ref, ups, ids, up)
    collect(me_ref, downs, ids, down)
    own = frames[0].shape[0]
    for index, piece in enumerate(frames):
        normed = normalise(piece[...].astype(F32))[0] * gain[...]
        normed_out[index * own : (index + 1) * own, :] = normed.astype(BF)
    pre = dot(normed_out[...], up[...], 1, 0)
    pre_out[...] = pre
    hidden_out[...] = (pre * jax.nn.sigmoid(pre)).astype(BF)
    made = dot(hidden_out[...], down[...], 1, 1)
    for index, out in enumerate(partials):
        out[...] = made[index * own : (index + 1) * own].astype(BF)


def mid_kernel(parts, *refs):
    gain, frames = refs[0], refs[1]
    pieces = refs[2 : 2 + parts]
    mid_out, normed_out = refs[2 + parts :]
    total = pieces[0][...].astype(F32)
    for piece in pieces[1:]:
        total = total + piece[...].astype(F32)
    mid = frames[...].astype(F32) + 0.5 * total
    mid_out[...] = mid
    normed_out[...] = (normalise(mid)[0] * gain[...]).astype(BF)


def attention_kernel(parts, ids, heads, window, cot_scale, *refs):
    count = len(ids)
    me_ref, bias = refs[0], refs[1]
    seg_q, span_q, seg_k, span_k = refs[2:6]
    at = 6
    normed_parts = refs[at : at + parts]
    at += parts
    cot_parts = refs[at : at + parts]
    at += parts
    pieces = refs[at : at + count]
    at += count
    normed, scaled, context, slopes = refs[at : at + 4]
    at += 4
    attn_outs = refs[at : at + parts]
    at += parts
    normed_outs = refs[at : at + parts]
    at += parts
    weights, qkv, grad_context, key_total, value_total = refs[at:]
    frames = normed.shape[0]
    own = normed_parts[0].shape[0]
    inner = weights.shape[1] // 4
    width = inner // heads
    scale = width ** (-0.5)
    for index in range(parts):
        rows = slice(index * own, (index + 1) * own)
        normed[rows, :] = normed_parts[index][...]
        scaled[rows, :] = (cot_parts[index][...].astype(F32) * cot_scale).astype(BF)
    collect(me_ref, pieces, ids, weights)
    qkv[...] = dot(normed[...], weights[:, : 3 * inner], 1, 0).astype(BF)
    grad_context[...] = dot(scaled[...], weights[:, 3 * inner :], 1, 0).astype(BF)
    block = min(frames, 256)
    reach = min(window, (frames - 1) // SPAN)
    for head in range(heads):
        cols = slice(head * width, (head + 1) * width)
        key_cols = slice(inner + head * width, inner + (head + 1) * width)
        value_cols = slice(2 * inner + head * width, 2 * inner + (head + 1) * width)
        key = qkv[:, key_cols]
        value = qkv[:, value_cols]
        if frames > block:
            key_total[...] = jnp.zeros_like(key_total)
            value_total[...] = jnp.zeros_like(value_total)

        def step(turn, carry):
            rows = pl.ds(pl.multiple_of(turn * block, block), block)
            query = qkv[rows, cols]
            distance = span_q[rows, :] - span_k[...]
            allowed = (seg_q[rows, :] == seg_k[...]) & (distance >= 0) & (distance <= window)
            added = jnp.full((block, frames), bias[head, 0], F32)
            for far in range(1, reach + 1):
                added = jnp.where(distance == far, bias[head, far], added)
            scores = dot(query, key, 1, 1) * scale + added
            scores = jnp.where(allowed, scores, -1e30)
            expo = jnp.exp(scores - jnp.max(scores, axis=-1, keepdims=True))
            soft = expo / jnp.sum(expo, axis=-1, keepdims=True)
            low = soft.astype(BF)
            context[rows, cols] = dot(low, value, 1, 0).astype(BF)
            slope = grad_context[rows, cols]
            probs = dot(slope, value, 1, 1)
            probs = probs - jnp.sum(soft * probs, axis=-1, keepdims=True)
            grad = (soft * probs).astype(BF)
            slopes[rows, cols] = (dot(grad, key, 1, 0) * scale).astype(BF)
            key_slope = dot(grad, query, 0, 0)
            value_slope = dot(low, slope, 0, 0)
            if frames > block:
                key_total[...] += key_slope
                value_total[...] += value_slope
            else:
                slopes[:, key_cols] = (key_slope * scale).astype(BF)
                slopes[:, value_cols] = value_slope.astype(BF)
            return carry

        if frames > block:
            lax.fori_loop(0, frames // block, step, 0)
            slopes[:, key_cols] = (key_total[...] * scale).astype(BF)
            slopes[:, value_cols] = value_total[...].astype(BF)
        else:
            step(0, 0)
    made = dot(slopes[...], weights[:, : 3 * inner], 1, 1)
    for index, out in enumerate(normed_outs):
        out[...] = made[index * own : (index + 1) * own].astype(BF)
    made = dot(context[...], weights[:, 3 * inner :], 1, 1)
    for index, out in enumerate(attn_outs):
        out[...] = made[index * own : (index + 1) * own].astype(BF)


def attention_grads_kernel(ids, *refs):
    count = len(ids)
    me_ref, normed, scaled, context, slopes = refs[:5]
    outs = refs[5 : 5 + count]
    total = refs[5 + count]
    inner = context.shape[1]
    for index in range(3):
        total[...] = dot(normed[...], slopes[:, index * inner : (index + 1) * inner], 0, 0)
        hand_out(me_ref, total, ids, outs, index * inner)
    total[...] = dot(scaled[...], context[...], 0, 0)
    hand_out(me_ref, total, ids, outs, 3 * inner)


def grad_mid_kernel(parts, cot_scale, *refs):
    gain, mid, cot = refs[:3]
    pieces = refs[3 : 3 + parts]
    out = refs[3 + parts]
    upstream = pieces[0][...].astype(F32)
    for piece in pieces[1:]:
        upstream = upstream + piece[...].astype(F32)
    normed, inverse = normalise(mid[...])
    scaled = upstream * gain[...]
    first = jnp.mean(scaled, axis=-1, keepdims=True)
    second = jnp.mean(scaled * normed, axis=-1, keepdims=True)
    slope = inverse * (scaled - first - normed * second)
    low_cot = (cot[...].astype(F32) * cot_scale).astype(BF).astype(F32)
    out[...] = (low_cot + slope).astype(BF)


def ffn_grads_kernel(parts, ids, *refs):
    count = len(ids)
    me_ref, normed, pre, hidden = refs[:4]
    mids = refs[4 : 4 + parts]
    downs = refs[4 + parts : 4 + parts + count]
    outs = refs[4 + parts + count : 4 + parts + 2 * count]
    down, grad_mid, total = refs[4 + parts + 2 * count :]
    own = mids[0].shape[0]
    collect(me_ref, downs, ids, down)
    for index, piece in enumerate(mids):
        grad_mid[index * own : (index + 1) * own, :] = piece[...]
    total[...] = 0.5 * dot(grad_mid[...], hidden[...], 0, 0)
    hand_out(me_ref, total, ids, outs, down.shape[1])
    sigma = jax.nn.sigmoid(pre[...])
    slope = sigma * (1.0 + pre[...] * (1.0 - sigma))
    grad_hidden = (0.5 * dot(grad_mid[...], down[...], 1, 0) * slope).astype(BF)
    total[...] = dot(normed[...], grad_hidden, 0, 0)
    hand_out(me_ref, total, ids, outs, 0)


def pair_sum_kernel(*refs):
    count = len(refs) // 3
    for index in range(count):
        total = refs[index][...].astype(F32) + refs[count + index][...].astype(F32)
        refs[2 * count + index][...] = total.astype(BF)


def per_device(
    frames_in,
    segment_ids,
    span_ids,
    ffn_gain,
    w_up,
    w_down,
    attn_gain,
    w_query,
    w_key,
    w_value,
    w_out,
    offset_bias,
    cotangent,
):
    dp, ctx = lax.axis_size("dp"), lax.axis_size("ctx")
    own, model = frames_in.shape[1:]
    frames = own * ctx
    heads = offset_bias.shape[0]
    window = offset_bias.shape[1] - 1
    hidden, inner = w_up.shape[1], w_query.shape[1]
    rows = w_up.shape[0]
    direct_rows = dp == 8 and rows % 16 == 0
    direct_frames = ctx == 4 and own % 16 == 0
    ids = (0, 2, 4, 6, 1, 3, 5, 7) if direct_rows else (0,)
    parts = ctx if direct_frames else 1
    part_rows = frames // parts
    me = lax.axis_index("dp").astype(jnp.int32).reshape(1)
    place = lax.axis_index("ctx")
    cot_scale = 1.0 / math.sqrt(dp * frames)

    def gather_rows(weight):
        if not direct_rows:
            return [lax.all_gather(weight, "dp", axis=0, tiled=True)]
        near = [weight] + [exchange(weight, "dp", mask) for mask in ids[1:4]]
        return near + [exchange(one, "dp", 1) for one in near]

    def gather_frames(values):
        if not direct_frames:
            return [lax.all_gather(values, "ctx", axis=0, tiled=True)]
        return [values] + [exchange(values, "ctx", mask) for mask in range(1, ctx)]

    def scatter_frames(pieces):
        if not direct_frames:
            return [lax.psum_scatter(pieces[0], "ctx", scatter_dimension=0, tiled=True)]
        return [pieces[0]] + [exchange(pieces[mask], "ctx", mask) for mask in range(1, ctx)]

    def scatter_rows(pieces):
        if not direct_rows:
            made = lax.psum_scatter(pieces[0], "dp", scatter_dimension=0, tiled=True)
            return made.astype(F32)
        came = [exchange(one, "dp", 1) for one in pieces[4:]]
        outs = [shape(one.shape, BF) for one in came]
        sums = call(pair_sum_kernel, outs, list(pieces[:4]) + came)
        total = sums[0].astype(F32)
        for one, mask in zip(sums[1:], ids[1:4]):
            total = total + exchange(one, "dp", mask).astype(F32)
        return total

    frames_own, cot_own = frames_in[0], cotangent[0]
    frame_parts = gather_frames(frames_own)
    ups, downs = gather_rows(w_up), gather_rows(w_down)
    attn_weights = jnp.concatenate([w_query, w_key, w_value, w_out], axis=1)
    attn_pieces = gather_rows(attn_weights)
    cot_parts = gather_frames(cot_own)

    segments, spans = segment_ids[0], span_ids[0]
    if direct_frames:
        order = place ^ jnp.arange(ctx, dtype=jnp.int32)
        segments = segments.reshape(ctx, own)[order].reshape(frames)
        spans = spans.reshape(ctx, own)[order].reshape(frames)
    marks = [
        segments.reshape(frames, 1),
        spans.reshape(frames, 1),
        segments.reshape(1, frames),
        spans.reshape(1, frames),
    ]
    ffn_gain = ffn_gain.reshape(1, model)
    attn_gain = attn_gain.reshape(1, model)

    made = call(
        functools.partial(ffn_kernel, parts, ids),
        [shape((frames, model), BF), shape((frames, hidden), F32), shape((frames, hidden), BF)]
        + [shape((part_rows, model), BF)] * parts,
        [me, ffn_gain] + frame_parts + ups + downs,
        [pltpu.VMEM((model, hidden), BF)] * 2,
        flops=4 * frames * model * hidden,
        smem=1,
    )
    ffn_normed, ffn_pre, ffn_hidden = made[:3]
    summed = scatter_frames(list(made[3:]))
    mid_own, normed_own = call(
        functools.partial(mid_kernel, len(summed)),
        [shape((own, model), F32), shape((own, model), BF)],
        [attn_gain, frames_own] + summed,
    )
    normed_parts = gather_frames(normed_own)
    made = call(
        functools.partial(attention_kernel, parts, ids, heads, window, cot_scale),
        [
            shape((frames, model), BF),
            shape((frames, model), BF),
            shape((frames, inner), BF),
            shape((frames, 3 * inner), BF),
        ]
        + [shape((part_rows, model), BF)] * (2 * parts),
        [me, offset_bias] + marks + normed_parts + cot_parts + attn_pieces,
        [
            pltpu.VMEM((model, 4 * inner), BF),
            pltpu.VMEM((frames, 3 * inner), BF),
            pltpu.VMEM((frames, inner), BF),
            pltpu.VMEM((frames, inner // heads), F32),
            pltpu.VMEM((frames, inner // heads), F32),
        ],
        flops=16 * frames * model * inner + 12 * frames * frames * inner,
        smem=2,
    )
    attn_normed, scaled_cot, context, slopes = made[:4]
    attn_partials = list(made[4 : 4 + parts])
    normed_partials = list(made[4 + parts :])
    upstream = scatter_frames(normed_partials)
    attn_grads = call(
        functools.partial(attention_grads_kernel, ids),
        [shape((model // len(ids), 4 * inner), BF)] * len(ids),
        [me, attn_normed, scaled_cot, context, slopes],
        [pltpu.VMEM((model, inner), F32)],
        flops=8 * frames * model * inner,
        smem=1,
    )
    attn_total = scatter_rows(attn_grads)
    (grad_mid_own,) = call(
        functools.partial(grad_mid_kernel, len(upstream), cot_scale),
        [shape((own, model), BF)],
        [attn_gain, mid_own, cot_own] + upstream,
    )
    grad_mid_parts = gather_frames(grad_mid_own)
    ffn_grads = call(
        functools.partial(ffn_grads_kernel, parts, ids),
        [shape((model // len(ids), 2 * hidden), BF)] * len(ids),
        [me, ffn_normed, ffn_pre, ffn_hidden] + grad_mid_parts + downs,
        [
            pltpu.VMEM((model, hidden), BF),
            pltpu.VMEM((frames, model), BF),
            pltpu.VMEM((model, hidden), F32),
        ],
        flops=6 * frames * model * hidden,
        smem=1,
    )
    attn_sum = sum(one.astype(F32) for one in scatter_frames(attn_partials))
    block_out = (mid_own + attn_sum).astype(BF)[None]
    ffn_total = scatter_rows(ffn_grads)
    return (
        block_out,
        ffn_total[:, :hidden],
        ffn_total[:, hidden:],
        attn_total[:, :inner],
        attn_total[:, inner : 2 * inner],
        attn_total[:, 2 * inner : 3 * inner],
        attn_total[:, 3 * inner :],
    )


def solution(mesh):
    placed = (
        P("dp", "ctx", None),
        P("dp", None),
        P("dp", None),
        P(),
        P("dp", "ctx"),
        P("dp", "ctx"),
        P(),
        P("dp", "ctx"),
        P("dp", "ctx"),
        P("dp", "ctx"),
        P("dp", "ctx"),
        P("ctx", None),
        P("dp", "ctx", None),
    )
    return jax.shard_map(
        per_device,
        mesh=mesh,
        in_specs=placed,
        out_specs=(P("dp", "ctx", None),) + (P("dp", "ctx"),) * 6,
        check_vma=False,
    )
```

```python
import functools
import math

import jax
import jax.numpy as jnp
from jax import lax
from jax.experimental import pallas as pl
from jax.experimental.pallas import tpu as pltpu
from jax.sharding import PartitionSpec as P

SPAN = 64
BF = jnp.bfloat16
F32 = jnp.float32
VMEM_BYTES = 56 * 1024 * 1024


def exchange(values, axis, mask):
    size = lax.axis_size(axis)
    return lax.ppermute(values, axis, [(one, one ^ mask) for one in range(size)])


def call(body, outs, args, scratch=(), flops=0, smem=0, after=()):
    count = len(args)
    specs = [pl.BlockSpec(memory_space=pltpu.SMEM)] * smem
    specs += [pl.BlockSpec(memory_space=pltpu.VMEM)] * (count - smem)
    specs += [pl.BlockSpec(memory_space=pl.ANY)] * len(after)
    moved = sum(math.prod(one.shape) * one.dtype.itemsize for one in list(args) + list(outs))
    return pl.pallas_call(
        lambda *refs: body(*refs[:count], *refs[count + len(after) :]),
        out_shape=tuple(outs),
        in_specs=specs,
        out_specs=tuple(pl.BlockSpec(memory_space=pltpu.VMEM) for _ in outs),
        scratch_shapes=list(scratch),
        compiler_params=pltpu.CompilerParams(vmem_limit_bytes=VMEM_BYTES),
        cost_estimate=pl.CostEstimate(flops=flops, bytes_accessed=moved, transcendentals=0),
    )(*args, *after)


def shape(dims, dtype):
    return jax.ShapeDtypeStruct(dims, dtype)


def dot(left, right, left_dim, right_dim):
    return lax.dot_general(
        left, right, (((left_dim,), (right_dim,)), ((), ())), preferred_element_type=F32
    )


def normalise(values):
    center = values - jnp.mean(values, axis=-1, keepdims=True)
    variance = jnp.mean(center * center, axis=-1, keepdims=True)
    inverse = lax.rsqrt(variance + 1e-05)
    return center * inverse, inverse


def collect(me_ref, pieces, ids, first_column, target):
    rows, width = target.shape
    rows = rows // len(ids)
    columns = slice(first_column, first_column + width)
    if len(ids) == 1:
        target[...] = pieces[0][:, columns]
        return
    blocks = [(piece, at) for piece in pieces for at in range(0, piece.shape[0], rows)]
    for (piece, at), mask in zip(blocks, ids):
        first = pl.multiple_of((me_ref[0] ^ mask) * rows, 16)
        target[pl.ds(first, rows), :] = piece[at : at + rows, columns]


def hand_out(me_ref, total, firsts, rows, outs, first_column):
    width = total.shape[1]
    columns = slice(first_column, first_column + width)
    if len(outs) == 1:
        outs[0][:, columns] = total[...].astype(BF)
        return
    blocks = [(out, at) for out in outs for at in range(0, out.shape[0], rows)]
    for (out, at), first in zip(blocks, firsts):
        block = total[pl.ds(pl.multiple_of(first * rows, 8), rows), :]
        out[at : at + rows, columns] = block.astype(BF)


def ffn_kernel(parts, ids, *refs):
    me_ref, gain = refs[:2]
    frames = refs[2 : 2 + parts]
    at = 2 + parts + (1 if len(ids) == 1 else 2)
    weights, rest = refs[2 + parts : at], refs[at:]
    normed_out, pre_out, hidden_out, down = rest[:4]
    partials = rest[4 : 4 + parts]
    up = rest[4 + parts]
    model, width = up.shape
    collect(me_ref, weights, ids, 0, up)
    collect(me_ref, weights, ids, width, down)
    own = frames[0].shape[0]
    for index, piece in enumerate(frames):
        normed = normalise(piece[:, :model].astype(F32))[0] * gain[...].reshape(1, -1)
        normed_out[index * own : (index + 1) * own, :] = normed.astype(BF)
    pre = dot(normed_out[...], up[...], 1, 0)
    pre_out[...] = pre
    hidden_out[...] = (pre * jax.nn.sigmoid(pre)).astype(BF)
    made = dot(hidden_out[...], down[...], 1, 1)
    for index, out in enumerate(partials):
        out[...] = made[index * own : (index + 1) * own].astype(BF)


def mid_kernel(parts, *refs):
    gain, frames = refs[0], refs[1]
    pieces = refs[2 : 2 + parts]
    stacked = (len(refs) - parts - 4) // 4 * 4
    weights = refs[2 + parts : 2 + parts + stacked]
    mid_out, normed_out = refs[2 + parts + stacked : 4 + parts + stacked]
    if stacked:
        stack_kernel(*weights, refs[-1])
    total = pieces[0][...].astype(F32)
    for piece in pieces[1:]:
        total = total + piece[...].astype(F32)
    mid = frames[...].astype(F32) + 0.5 * total
    mid_out[...] = mid
    normed_out[...] = (normalise(mid)[0] * gain[...].reshape(1, -1)).astype(BF)


def attention_kernel(parts, ids, window, cot_scale, *refs):
    place_ref, me_ref, bias = refs[:3]
    segments, spans = refs[3:5]
    normed_parts = refs[5 : 5 + parts]
    cot_parts = refs[5 + parts : 5 + 2 * parts]
    at = 5 + 2 * parts + (1 if len(ids) == 1 else 2)
    weights_in, rest = refs[5 + 2 * parts : at], refs[at:]
    normed, scaled, context, slopes = rest[:4]
    attn_out, outs = rest[4], rest[5 : 5 + parts]
    weights, qkv, grad_context, key_total, value_total, total = rest[5 + parts :]
    heads = bias.shape[0]
    frames = normed.shape[0]
    own = normed_parts[0].shape[0]
    inner = context.shape[1]
    width = inner // heads
    scale = width ** (-0.5)
    firsts = [0]
    if parts > 1:
        firsts = [pl.multiple_of((place_ref[0] ^ mask) * own, 16) for mask in range(parts)]
    for first, piece, both in zip(firsts, normed_parts, cot_parts):
        normed[pl.ds(first, own), :] = piece[...]
        cot = both[:, normed.shape[1] :].astype(F32)
        scaled[pl.ds(first, own), :] = (cot * cot_scale).astype(BF)
    collect(me_ref, weights_in, ids, 0, weights)
    qkv[...] = dot(normed[...], weights[:, : 3 * inner], 1, 0).astype(BF)
    grad_context[...] = dot(scaled[...], weights[:, 3 * inner :], 1, 0).astype(BF)
    seg_k, span_k = segments[...], spans[...]
    seg_q = jnp.transpose(jnp.broadcast_to(seg_k, (8, frames)))[:, :1]
    span_q = jnp.transpose(jnp.broadcast_to(span_k, (8, frames)))[:, :1]
    block = min(frames, 256)
    reach = min(window, (frames - 1) // SPAN)
    for head in range(heads):
        cols = slice(head * width, (head + 1) * width)
        key_cols = slice(inner + head * width, inner + (head + 1) * width)
        value_cols = slice(2 * inner + head * width, 2 * inner + (head + 1) * width)
        key = qkv[:, key_cols]
        value = qkv[:, value_cols]
        for first in range(0, frames, block):
            mine = slice(first, first + block)
            query = qkv[mine, cols]
            distance = span_q[mine, :] - span_k
            allowed = (seg_q[mine, :] == seg_k) & (distance >= 0) & (distance <= window)
            added = jnp.full((block, frames), bias[head, 0], F32)
            for far in range(1, reach + 1):
                added = jnp.where(distance == far, bias[head, far], added)
            scores = dot(query, key, 1, 1) * scale + added
            scores = jnp.where(allowed, scores, -1e30)
            expo = jnp.exp(scores - jnp.max(scores, axis=-1, keepdims=True))
            soft = expo / jnp.sum(expo, axis=-1, keepdims=True)
            low = soft.astype(BF)
            context[mine, cols] = dot(low, value, 1, 0).astype(BF)
            slope = grad_context[mine, cols]
            probs = dot(slope, value, 1, 1)
            probs = probs - jnp.sum(soft * probs, axis=-1, keepdims=True)
            grad = (soft * probs).astype(BF)
            slopes[mine, cols] = (dot(grad, key, 1, 0) * scale).astype(BF)
            key_slope = dot(grad, query, 0, 0)
            value_slope = dot(low, slope, 0, 0)
            if first > 0:
                key_slope = key_total[...] + key_slope
                value_slope = value_total[...] + value_slope
            if first + block < frames:
                key_total[...] = key_slope
                value_total[...] = value_slope
        slopes[:, key_cols] = (key_slope * scale).astype(BF)
        slopes[:, value_cols] = value_slope.astype(BF)
    total[...] = dot(slopes[...], weights[:, : 3 * inner], 1, 1)
    for first, out in zip(firsts, outs):
        out[...] = total[pl.ds(first, own), :].astype(BF)
    total[...] = dot(context[...], weights[:, 3 * inner :], 1, 1)
    attn_out[...] = total[...].astype(BF)


def attention_grads_kernel(*refs):
    me_ref, normed, scaled, context, slopes = refs[:5]
    outs, total = refs[5:-1], refs[-1]
    inner = context.shape[1]
    rows = total.shape[0] // 8
    firsts = [me_ref[0] ^ mask for mask in (0, 2, 4, 6, 1, 3, 5, 7)]
    for index in range(3):
        total[...] = dot(normed[...], slopes[:, index * inner : (index + 1) * inner], 0, 0)
        hand_out(me_ref, total, firsts, rows, outs, index * inner)
    total[...] = dot(scaled[...], context[...], 0, 0)
    hand_out(me_ref, total, firsts, rows, outs, 3 * inner)


def grad_mid_kernel(parts, cot_scale, *refs):
    gain, mid, cot = refs[:3]
    pieces = refs[3 : 3 + parts]
    out = refs[3 + parts]
    upstream = pieces[0][...].astype(F32)
    for piece in pieces[1:]:
        upstream = upstream + piece[...].astype(F32)
    normed, inverse = normalise(mid[...])
    scaled = upstream * gain[...].reshape(1, -1)
    first = jnp.mean(scaled, axis=-1, keepdims=True)
    second = jnp.mean(scaled * normed, axis=-1, keepdims=True)
    slope = inverse * (scaled - first - normed * second)
    low_cot = (cot[...].astype(F32) * cot_scale).astype(BF).astype(F32)
    out[...] = (low_cot + slope).astype(BF)


def ffn_grads_kernel(parts, *refs):
    me_ref, normed, pre, hidden, down = refs[:5]
    mids = refs[5 : 5 + parts]
    outs = refs[5 + parts : -2]
    grad_mid, total = refs[-2:]
    own = mids[0].shape[0]
    rows = total.shape[0] // 8
    firsts = [me_ref[0] ^ mask for mask in (0, 2, 4, 6, 1, 3, 5, 7)]
    for index, piece in enumerate(mids):
        grad_mid[index * own : (index + 1) * own, :] = piece[...]
    total[...] = 0.5 * dot(grad_mid[...], hidden[...], 0, 0)
    hand_out(me_ref, total, firsts, rows, outs, down.shape[1])
    sigma = jax.nn.sigmoid(pre[...])
    slope = sigma * (1.0 + pre[...] * (1.0 - sigma))
    grad_hidden = (0.5 * dot(grad_mid[...], down[...], 1, 0) * slope).astype(BF)
    total[...] = dot(normed[...], grad_hidden, 0, 0)
    hand_out(me_ref, total, firsts, rows, outs, 0)


def pair_sum_kernel(keep, came, *refs):
    passed = (len(refs) - 4) // 2
    rows = keep.shape[0] // 4
    for at, out in enumerate(refs[passed : passed + 4]):
        mine = slice(at * rows, (at + 1) * rows)
        out[...] = (keep[mine, :].astype(F32) + came[mine, :].astype(F32)).astype(BF)
    for one, out in zip(refs[:passed], refs[passed + 4 :]):
        out[...] = one[...]


def pack_kernel(*refs):
    out, at = refs[-1], 0
    for piece in refs[:-1]:
        out[:, at : at + piece.shape[1]] = piece[...]
        at += piece.shape[1]


def pack(pieces, after=()):
    total = sum(one.shape[1] for one in pieces)
    return call(pack_kernel, [shape((pieces[0].shape[0], total), BF)], pieces, after=after)[0]


def stack_kernel(*refs):
    out, at = refs[-1], 0
    for piece in refs[:-1]:
        out[at : at + piece.shape[0], :] = piece[...]
        at += piece.shape[0]


def stack(pieces, after=()):
    total = sum(one.shape[0] for one in pieces)
    return call(stack_kernel, [shape((total, pieces[0].shape[1]), BF)], pieces, after=after)[0]


def per_device(
    frames_in,
    segment_ids,
    span_ids,
    ffn_gain,
    w_up,
    w_down,
    attn_gain,
    w_query,
    w_key,
    w_value,
    w_out,
    offset_bias,
    cotangent,
):
    dp, ctx = lax.axis_size("dp"), lax.axis_size("ctx")
    own, model = frames_in.shape[1:]
    frames = own * ctx
    heads = offset_bias.shape[0]
    window = offset_bias.shape[1] - 1
    hidden, inner = w_up.shape[1], w_query.shape[1]
    rows = w_up.shape[0]
    direct_rows = dp == 8 and rows % 16 == 0
    direct_frames = ctx == 4 and own % 16 == 0
    ids = (0, 6, 4, 2, 1, 7, 5, 3) if direct_rows else (0,)
    parts = ctx if direct_frames else 1
    part_rows = frames // parts
    me = lax.axis_index("dp").astype(jnp.int32).reshape(1)
    place = lax.axis_index("ctx").astype(jnp.int32).reshape(1)
    cot_scale = 1.0 / math.sqrt(dp * frames)

    def gather_frames(values):
        if not direct_frames:
            return [lax.all_gather(values, "ctx", axis=0, tiled=True)]
        return [values] + [exchange(values, "ctx", mask) for mask in (1, 2, 3)]

    def scatter_frames(pieces):
        if not direct_frames:
            return [lax.psum_scatter(pieces[0], "ctx", scatter_dimension=0, tiled=True)]
        return [pieces[0]] + [exchange(pieces[mask], "ctx", mask) for mask in (1, 2, 3)]

    def scatter_rows(pieces, passed=()):
        if not direct_rows:
            made = lax.psum_scatter(pieces[0], "dp", scatter_dimension=0, tiled=True)
            return [made], passed
        keep, send = pieces
        came = exchange(send, "dp", 1)
        outs = [shape((rows, keep.shape[1]), BF)] * 4 + [shape(one.shape, BF) for one in passed]
        sums = call(pair_sum_kernel, outs, [keep, came, *passed])
        terms = [sums[0]] + [exchange(sums[at], "dp", 2 * at) for at in (1, 2, 3)]
        return terms, sums[4:] if passed else sums[:1]

    def add_terms(terms):
        total = terms[0].astype(F32)
        for one in terms[1:]:
            total = total + one.astype(F32)
        return total

    frames_own, cot_own = frames_in[0], cotangent[0]
    both_parts = gather_frames(pack([frames_own, cot_own]))

    def gather_near(weight):
        return [weight] + [exchange(weight, "dp", mask) for mask in (6, 4, 2)]

    if direct_rows:
        ffn_near = stack(gather_near(pack([w_up, w_down])), both_parts[1:])
        ffn_weights = [ffn_near, exchange(ffn_near, "dp", 1)]
        attn_pieces = gather_near(pack([w_query, w_key, w_value, w_out], [ffn_near]))
    else:
        ffn_weights = [lax.all_gather(pack([w_up, w_down]), "dp", axis=0, tiled=True)]
        attn_weights = pack([w_query, w_key, w_value, w_out])
        attn_weights = [lax.all_gather(attn_weights, "dp", axis=0, tiled=True)]
        attn_pieces = []

    made = call(
        functools.partial(ffn_kernel, parts, ids),
        [
            shape((frames, model), BF),
            shape((frames, hidden), F32),
            shape((frames, hidden), BF),
            shape((model, hidden), BF),
        ]
        + [shape((part_rows, model), BF)] * parts,
        [me, ffn_gain] + both_parts + ffn_weights,
        [pltpu.VMEM((model, hidden), BF)],
        flops=4 * frames * model * hidden,
        smem=1,
    )
    ffn_normed, ffn_pre, ffn_hidden, down_full = made[:4]
    summed = scatter_frames(list(made[4:]))
    near = [shape((model // 2, 4 * inner), BF)] if direct_rows else []
    mid_own, normed_own, *near = call(
        functools.partial(mid_kernel, len(summed)),
        [shape((own, model), F32), shape((own, model), BF)] + near,
        [attn_gain, frames_own] + summed + attn_pieces,
    )
    normed_parts = gather_frames(normed_own)
    if direct_rows:
        attn_weights = [near[0], exchange(near[0], "dp", 1)]
    made = call(
        functools.partial(attention_kernel, parts, ids, window, cot_scale),
        [
            shape((frames, model), BF),
            shape((frames, model), BF),
            shape((frames, inner), BF),
            shape((frames, 3 * inner), BF),
            shape((frames, model), BF),
        ]
        + [shape((part_rows, model), BF)] * parts,
        [place, me, offset_bias, segment_ids, span_ids] + normed_parts + both_parts + attn_weights,
        [
            pltpu.VMEM((model, 4 * inner), BF),
            pltpu.VMEM((frames, 3 * inner), BF),
            pltpu.VMEM((frames, inner), BF),
            pltpu.VMEM((frames, inner // heads), F32),
            pltpu.VMEM((frames, inner // heads), F32),
            pltpu.VMEM((frames, model), F32),
        ],
        flops=16 * frames * model * inner + 12 * frames * frames * inner,
        smem=3,
    )
    attn_normed, scaled_cot, context, slopes = made[:4]
    attn_partial = made[4]
    upstream = scatter_frames(list(made[5:]))
    half = [shape((model // 2, 4 * inner), BF)] * 2
    attn_grads = call(
        attention_grads_kernel,
        half if direct_rows else [shape((model, 4 * inner), BF)],
        [me, attn_normed, scaled_cot, context, slopes],
        [pltpu.VMEM((model, inner), F32)],
        flops=8 * frames * model * inner,
        smem=1,
    )
    (grad_mid_own,) = call(
        functools.partial(grad_mid_kernel, len(upstream), cot_scale),
        [shape((own, model), BF)],
        [attn_gain, mid_own, cot_own] + upstream,
    )
    grad_mid_parts = gather_frames(grad_mid_own)
    attn_terms, attn_sums = scatter_rows(attn_grads)
    half = [shape((model // 2, 2 * hidden), BF)] * 2
    ffn_grads = call(
        functools.partial(ffn_grads_kernel, parts),
        half if direct_rows else [shape((model, 2 * hidden), BF)],
        [me, ffn_normed, ffn_pre, ffn_hidden, down_full] + grad_mid_parts,
        [pltpu.VMEM((frames, model), BF), pltpu.VMEM((model, hidden), F32)],
        flops=6 * frames * model * hidden,
        smem=1,
        after=attn_sums,
    )
    ffn_terms, passed = scatter_rows(ffn_grads, [attn_partial])
    if direct_frames:
        attn_sum = lax.all_to_all(passed[0], "ctx", 0, 0, tiled=True)
        attn_sum = add_terms([attn_sum[at * own : (at + 1) * own] for at in range(ctx)])
    else:
        attn_sum = lax.psum_scatter(passed[0], "ctx", scatter_dimension=0, tiled=True)
    block_out = (mid_own + attn_sum).astype(BF)[None]
    attn_total, ffn_total = add_terms(attn_terms), add_terms(ffn_terms)
    return (
        block_out,
        ffn_total[:, :hidden],
        ffn_total[:, hidden:],
        attn_total[:, :inner],
        attn_total[:, inner : 2 * inner],
        attn_total[:, 2 * inner : 3 * inner],
        attn_total[:, 3 * inner :],
    )


def solution(mesh):
    placed = (
        P("dp", "ctx", None),
        P("dp", None),
        P("dp", None),
        P(),
        P("dp", "ctx"),
        P("dp", "ctx"),
        P(),
        P("dp", "ctx"),
        P("dp", "ctx"),
        P("dp", "ctx"),
        P("dp", "ctx"),
        P("ctx", None),
        P("dp", "ctx", None),
    )
    return jax.shard_map(
        per_device,
        mesh=mesh,
        in_specs=placed,
        out_specs=(P("dp", "ctx", None),) + (P("dp", "ctx"),) * 6,
        check_vma=False,
    )
```

```python
import functools
import math

import jax
import jax.numpy as jnp
from jax import lax
from jax.experimental import pallas as pl
from jax.experimental.pallas import tpu as pltpu
from jax.sharding import PartitionSpec as P

SPAN = 64
BF = jnp.bfloat16
F32 = jnp.float32
MIB = 1024 * 1024


def exchange(values, axis, mask):
    size = lax.axis_size(axis)
    return lax.ppermute(values, axis, [(one, one ^ mask) for one in range(size)])


def call(body, outs, args, scratch=(), flops=0, smem=0, far=0, after=()):
    count = len(args)
    specs = [pl.BlockSpec(memory_space=pltpu.SMEM)] * smem
    specs += [pl.BlockSpec(memory_space=pltpu.VMEM)] * (count - smem - far)
    specs += [pl.BlockSpec(memory_space=pl.ANY)] * (far + len(after))
    moved = sum(math.prod(one.shape) * one.dtype.itemsize for one in list(args) + list(outs))
    held = moved + sum(math.prod(one.shape) * jnp.dtype(one.dtype).itemsize for one in scratch)
    if far:
        scratch = [*scratch, pltpu.SemaphoreType.DMA((16,))]
    return pl.pallas_call(
        lambda *refs: body(*refs[:count], *refs[count + len(after) :]),
        out_shape=tuple(outs),
        in_specs=specs,
        out_specs=tuple(pl.BlockSpec(memory_space=pltpu.VMEM) for _ in outs),
        scratch_shapes=list(scratch),
        compiler_params=pltpu.CompilerParams(vmem_limit_bytes=min(held + 6 * MIB, 56 * MIB)),
        cost_estimate=pl.CostEstimate(flops=flops, bytes_accessed=moved, transcendentals=0),
    )(*args, *after)


def shape(dims, dtype):
    return jax.ShapeDtypeStruct(dims, dtype)


def dot(left, right, left_dim, right_dim):
    return lax.dot_general(
        left, right, (((left_dim,), (right_dim,)), ((), ())), preferred_element_type=F32
    )


def normalise(values):
    center = values - jnp.mean(values, axis=-1, keepdims=True)
    variance = jnp.mean(center * center, axis=-1, keepdims=True)
    inverse = lax.rsqrt(variance + 1e-05)
    return center * inverse, inverse


def start_copies(pairs, sems, first_sem=0):
    copies = []
    for at, (source, target) in enumerate(pairs):
        copies.append(pltpu.make_async_copy(source, target, sems.at[first_sem + at]))
        copies[-1].start()
    return copies


def wait_copies(copies):
    for one in copies:
        one.wait()


def collect(me_ref, pieces, ids, first_column, target, sems, first_sem=0):
    rows, width = target.shape
    rows = rows // len(ids)
    columns = slice(first_column, first_column + width)
    if len(ids) == 1:
        target[...] = pieces[0][:, columns]
        return []
    blocks = [(piece, at) for piece in pieces for at in range(0, piece.shape[0], rows)]
    pairs = []
    for (piece, at), mask in zip(blocks, ids):
        first = pl.multiple_of((me_ref[0] ^ mask) * rows, 16)
        source = piece.at[pl.ds(at, rows), pl.ds(first_column, width)]
        pairs.append((source, target.at[pl.ds(first, rows), :]))
    return start_copies(pairs, sems, first_sem)


def hand_out(me_ref, total, firsts, rows, outs, first_column):
    width = total.shape[1]
    columns = slice(first_column, first_column + width)
    if len(outs) == 1:
        outs[0][:, columns] = total[...].astype(BF)
        return
    blocks = [(out, at) for out in outs for at in range(0, out.shape[0], rows)]
    for (out, at), first in zip(blocks, firsts):
        block = total[pl.ds(pl.multiple_of(first * rows, 8), rows), :]
        out[at : at + rows, columns] = block.astype(BF)


def ffn_kernel(parts, ids, cot_scale, *refs):
    place_ref, me_ref, gain = refs[:3]
    both_parts = refs[3 : 3 + parts]
    direct = len(ids) > 1
    at = 3 + parts + (2 if direct else 1)
    weights, rest = refs[3 + parts : at], refs[at:]
    normed_out, pre_out, hidden_out, down, scaled = rest[:5]
    partials = rest[5 : 5 + parts]
    up = rest[5 + parts]
    sems = rest[-1]
    model, width = up.shape
    up_copies = collect(me_ref, weights, ids, 0, up, sems)
    down_copies = collect(me_ref, weights, ids, width, down, sems, 8)
    own = both_parts[0].shape[0]
    for index, (first, both) in enumerate(zip(places(place_ref, parts, own), both_parts)):
        normed = normalise(both[:, :model].astype(F32))[0] * gain[...].reshape(1, -1)
        normed_out[index * own : (index + 1) * own, :] = normed.astype(BF)
        cot = both[:, model:].astype(F32)
        scaled[pl.ds(first, own), :] = (cot * cot_scale).astype(BF)
    wait_copies(up_copies)
    pre = dot(normed_out[...], up[...], 1, 0)
    pre_out[...] = pre
    hidden_out[...] = (pre * jax.nn.sigmoid(pre)).astype(BF)
    wait_copies(down_copies)
    made = dot(hidden_out[...], down[...], 1, 1)
    for index, out in enumerate(partials):
        out[...] = made[index * own : (index + 1) * own].astype(BF)


def places(place_ref, parts, own):
    if parts == 1:
        return [0]
    return [pl.multiple_of((place_ref[0] ^ mask) * own, 16) for mask in range(parts)]


def mid_kernel(parts, *refs):
    gain, frames = refs[0], refs[1]
    pieces = refs[2 : 2 + parts]
    stacked = 4 if len(refs) > parts + 4 else 0
    weights = refs[2 + parts : 2 + parts + stacked]
    mid_out, normed_out = refs[2 + parts + stacked : 4 + parts + stacked]
    copies = []
    if stacked:
        near, sems = refs[-2:]
        copies = start_copies(row_pairs(weights, near), sems)
    total = pieces[0][...].astype(F32)
    for piece in pieces[1:]:
        total = total + piece[...].astype(F32)
    mid = frames[...].astype(F32) + 0.5 * total
    mid_out[...] = mid
    normed_out[...] = (normalise(mid)[0] * gain[...].reshape(1, -1)).astype(BF)
    wait_copies(copies)


def attention_kernel(parts, ids, window, *refs):
    place_ref, me_ref, bias = refs[:3]
    segments, spans = refs[3:5]
    normed_parts = refs[5 : 5 + parts]
    scaled = refs[5 + parts]
    at = 6 + parts + (2 if len(ids) > 1 else 1)
    weights_in, rest = refs[6 + parts : at], refs[at:]
    normed, context, slopes = rest[:3]
    attn_out, outs = rest[3], rest[4 : 4 + parts]
    weights, qkv, grad_context, key_total, value_total, total = rest[4 + parts : 10 + parts]
    copies = collect(me_ref, weights_in, ids, 0, weights, rest[-1])
    heads = bias.shape[0]
    frames = normed.shape[0]
    own = normed_parts[0].shape[0]
    inner = context.shape[1]
    width = inner // heads
    scale = width ** (-0.5)
    firsts = places(place_ref, parts, own)
    for first, piece in zip(firsts, normed_parts):
        normed[pl.ds(first, own), :] = piece[...]
    wait_copies(copies)
    qkv[...] = dot(normed[...], weights[:, : 3 * inner], 1, 0).astype(BF)
    grad_context[...] = dot(scaled[...], weights[:, 3 * inner :], 1, 0).astype(BF)
    seg_k, span_k = segments[...], spans[...]
    seg_q = jnp.transpose(jnp.broadcast_to(seg_k, (8, frames)))[:, :1]
    span_q = jnp.transpose(jnp.broadcast_to(span_k, (8, frames)))[:, :1]
    block = min(frames, 256)
    reach = min(window, (frames - 1) // SPAN)
    for head in range(heads):
        cols = slice(head * width, (head + 1) * width)
        key_cols = slice(inner + head * width, inner + (head + 1) * width)
        value_cols = slice(2 * inner + head * width, 2 * inner + (head + 1) * width)
        key = qkv[:, key_cols]
        value = qkv[:, value_cols]
        for first in range(0, frames, block):
            mine = slice(first, first + block)
            query = qkv[mine, cols]
            distance = span_q[mine, :] - span_k
            allowed = (seg_q[mine, :] == seg_k) & (distance >= 0) & (distance <= window)
            added = jnp.full((block, frames), bias[head, 0], F32)
            for far in range(1, reach + 1):
                added = jnp.where(distance == far, bias[head, far], added)
            scores = dot(query, key, 1, 1) * scale + added
            scores = jnp.where(allowed, scores, -1e30)
            expo = jnp.exp(scores - jnp.max(scores, axis=-1, keepdims=True))
            soft = expo / jnp.sum(expo, axis=-1, keepdims=True)
            low = soft.astype(BF)
            context[mine, cols] = dot(low, value, 1, 0).astype(BF)
            slope = grad_context[mine, cols]
            probs = dot(slope, value, 1, 1)
            probs = probs - jnp.sum(soft * probs, axis=-1, keepdims=True)
            grad = (soft * probs).astype(BF)
            slopes[mine, cols] = (dot(grad, key, 1, 0) * scale).astype(BF)
            key_slope = dot(grad, query, 0, 0)
            value_slope = dot(low, slope, 0, 0)
            if first > 0:
                key_slope = key_total[...] + key_slope
                value_slope = value_total[...] + value_slope
            if first + block < frames:
                key_total[...] = key_slope
                value_total[...] = value_slope
        slopes[:, key_cols] = (key_slope * scale).astype(BF)
        slopes[:, value_cols] = value_slope.astype(BF)
    total[...] = dot(slopes[...], weights[:, : 3 * inner], 1, 1)
    for first, out in zip(firsts, outs):
        out[...] = total[pl.ds(first, own), :].astype(BF)
    total[...] = dot(context[...], weights[:, 3 * inner :], 1, 1)
    attn_out[...] = total[...].astype(BF)


def attention_grads_kernel(*refs):
    me_ref, normed, scaled, context, slopes = refs[:5]
    outs, total = refs[5:-1], refs[-1]
    inner = context.shape[1]
    rows = total.shape[0] // 8
    firsts = [me_ref[0] ^ mask for mask in (0, 2, 4, 6, 1, 3, 5, 7)]
    for index in range(3):
        total[...] = dot(normed[...], slopes[:, index * inner : (index + 1) * inner], 0, 0)
        hand_out(me_ref, total, firsts, rows, outs, index * inner)
    total[...] = dot(scaled[...], context[...], 0, 0)
    hand_out(me_ref, total, firsts, rows, outs, 3 * inner)


def grad_mid_kernel(parts, cot_scale, *refs):
    gain, mid, cot = refs[:3]
    pieces = refs[3 : 3 + parts]
    out = refs[3 + parts]
    upstream = pieces[0][...].astype(F32)
    for piece in pieces[1:]:
        upstream = upstream + piece[...].astype(F32)
    normed, inverse = normalise(mid[...])
    scaled = upstream * gain[...].reshape(1, -1)
    first = jnp.mean(scaled, axis=-1, keepdims=True)
    second = jnp.mean(scaled * normed, axis=-1, keepdims=True)
    slope = inverse * (scaled - first - normed * second)
    low_cot = (cot[...].astype(F32) * cot_scale).astype(BF).astype(F32)
    out[...] = (low_cot + slope).astype(BF)


def ffn_grads_kernel(parts, *refs):
    me_ref, normed, pre, hidden, down = refs[:5]
    mids = refs[5 : 5 + parts]
    outs = refs[5 + parts : -2]
    grad_mid, total = refs[-2:]
    own = mids[0].shape[0]
    rows = total.shape[0] // 8
    firsts = [me_ref[0] ^ mask for mask in (0, 2, 4, 6, 1, 3, 5, 7)]
    for index, piece in enumerate(mids):
        grad_mid[index * own : (index + 1) * own, :] = piece[...]
    total[...] = 0.5 * dot(grad_mid[...], hidden[...], 0, 0)
    hand_out(me_ref, total, firsts, rows, outs, down.shape[1])
    sigma = jax.nn.sigmoid(pre[...])
    slope = sigma * (1.0 + pre[...] * (1.0 - sigma))
    grad_hidden = (0.5 * dot(grad_mid[...], down[...], 1, 0) * slope).astype(BF)
    total[...] = dot(normed[...], grad_hidden, 0, 0)
    hand_out(me_ref, total, firsts, rows, outs, 0)


def pair_sum_kernel(keep, came, *refs):
    passed = (len(refs) - 4) // 2
    rows = keep.shape[0] // 4
    for at, out in enumerate(refs[passed : passed + 4]):
        mine = slice(at * rows, (at + 1) * rows)
        out[...] = (keep[mine, :].astype(F32) + came[mine, :].astype(F32)).astype(BF)
    for one, out in zip(refs[:passed], refs[passed + 4 :]):
        out[...] = one[...]


def row_pairs(pieces, out):
    starts = [sum(one.shape[0] for one in pieces[:at]) for at in range(len(pieces))]
    return [(one, out.at[pl.ds(at, one.shape[0]), :]) for one, at in zip(pieces, starts)]


def column_pairs(pieces, out):
    starts = [sum(one.shape[1] for one in pieces[:at]) for at in range(len(pieces))]
    return [(one, out.at[:, pl.ds(at, one.shape[1])]) for one, at in zip(pieces, starts)]


def stack_kernel(*refs):
    wait_copies(start_copies(row_pairs(refs[:-2], refs[-2]), refs[-1]))


def pack_kernel(groups, *refs):
    outs, pairs, at = refs[sum(groups) : -1], [], 0
    for count, out in zip(groups, outs):
        pairs += column_pairs(refs[at : at + count], out)
        at += count
    wait_copies(start_copies(pairs, refs[-1]))


def stack(pieces, after=()):
    total = sum(one.shape[0] for one in pieces)
    out = shape((total, pieces[0].shape[1]), BF)
    return call(stack_kernel, [out], pieces, far=len(pieces), after=after)[0]


def pack(groups, after=()):
    outs = [
        shape((group[0].shape[0], sum(one.shape[1] for one in group)), BF) for group in groups
    ]
    whole = all(one.shape[0] % 16 == 0 and one.shape[1] % 128 == 0 for group in groups for one in group)
    if not whole:
        return [jnp.concatenate(group, axis=1) for group in groups]
    pieces = [one for group in groups for one in group]
    body = functools.partial(pack_kernel, tuple(len(group) for group in groups))
    return call(body, outs, pieces, far=len(pieces), after=after)


def per_device(
    frames_in,
    segment_ids,
    span_ids,
    ffn_gain,
    w_up,
    w_down,
    attn_gain,
    w_query,
    w_key,
    w_value,
    w_out,
    offset_bias,
    cotangent,
):
    dp, ctx = lax.axis_size("dp"), lax.axis_size("ctx")
    own, model = frames_in.shape[1:]
    frames = own * ctx
    heads = offset_bias.shape[0]
    window = offset_bias.shape[1] - 1
    hidden, inner = w_up.shape[1], w_query.shape[1]
    rows = w_up.shape[0]
    direct_rows = dp == 8 and rows % 16 == 0
    direct_frames = ctx == 4 and own % 16 == 0
    ids = (0, 6, 4, 2, 1, 7, 5, 3) if direct_rows else (0,)
    parts = ctx if direct_frames else 1
    part_rows = frames // parts
    me = lax.axis_index("dp").astype(jnp.int32).reshape(1)
    place = lax.axis_index("ctx").astype(jnp.int32).reshape(1)
    cot_scale = 1.0 / math.sqrt(dp * frames)

    def gather_frames(values):
        if not direct_frames:
            return [lax.all_gather(values, "ctx", axis=0, tiled=True)]
        return [values] + [exchange(values, "ctx", mask) for mask in (1, 2, 3)]

    def scatter_frames(pieces):
        if not direct_frames:
            return [lax.psum_scatter(pieces[0], "ctx", scatter_dimension=0, tiled=True)]
        return [pieces[0]] + [exchange(pieces[mask], "ctx", mask) for mask in (1, 2, 3)]

    def scatter_rows(pieces, passed=()):
        if not direct_rows:
            made = lax.psum_scatter(pieces[0], "dp", scatter_dimension=0, tiled=True)
            return [made], passed
        keep, send = pieces
        came = exchange(send, "dp", 1)
        outs = [shape((rows, keep.shape[1]), BF)] * 4 + [shape(one.shape, BF) for one in passed]
        sums = call(pair_sum_kernel, outs, [keep, came, *passed])
        terms = [sums[0]] + [exchange(sums[at], "dp", 2 * at) for at in (1, 2, 3)]
        return terms, sums[4:] if passed else sums[:1]

    def add_terms(terms):
        total = terms[0].astype(F32)
        for one in terms[1:]:
            total = total + one.astype(F32)
        return total

    frames_own, cot_own = frames_in[0], cotangent[0]
    both_own, ffn_rows = pack([[frames_own, cot_own], [w_up, w_down]])
    both_parts = gather_frames(both_own)

    def gather_near(weight):
        return [weight] + [exchange(weight, "dp", mask) for mask in (6, 4, 2)]

    if direct_rows:
        ffn_near = stack(gather_near(ffn_rows), both_parts[1:])
        ffn_weights = [ffn_near, exchange(ffn_near, "dp", 1)]
        attn_pieces = gather_near(pack([[w_query, w_key, w_value, w_out]], [ffn_near])[0])
    else:
        ffn_weights = [lax.all_gather(ffn_rows, "dp", axis=0, tiled=True)]
        attn_weights = pack([[w_query, w_key, w_value, w_out]])[0]
        attn_weights = [lax.all_gather(attn_weights, "dp", axis=0, tiled=True)]
        attn_pieces = []

    made = call(
        functools.partial(ffn_kernel, parts, ids, cot_scale),
        [
            shape((frames, model), BF),
            shape((frames, hidden), F32),
            shape((frames, hidden), BF),
            shape((model, hidden), BF),
            shape((frames, model), BF),
        ]
        + [shape((part_rows, model), BF)] * parts,
        [place, me, ffn_gain] + both_parts + ffn_weights,
        [pltpu.VMEM((model, hidden), BF)],
        flops=4 * frames * model * hidden,
        smem=2,
        far=2 if direct_rows else 0,
    )
    ffn_normed, ffn_pre, ffn_hidden, down_full, scaled_cot = made[:5]
    summed = scatter_frames(list(made[5:]))
    near = [shape((model // 2, 4 * inner), BF)] if direct_rows else []
    mid_own, normed_own, *near = call(
        functools.partial(mid_kernel, len(summed)),
        [shape((own, model), F32), shape((own, model), BF)] + near,
        [attn_gain, frames_own] + summed + attn_pieces,
        far=len(attn_pieces),
    )
    normed_parts = gather_frames(normed_own)
    if direct_rows:
        attn_weights = [near[0], exchange(near[0], "dp", 1)]
    made = call(
        functools.partial(attention_kernel, parts, ids, window),
        [
            shape((frames, model), BF),
            shape((frames, inner), BF),
            shape((frames, 3 * inner), BF),
            shape((frames, model), BF),
        ]
        + [shape((part_rows, model), BF)] * parts,
        [place, me, offset_bias, segment_ids, span_ids] + normed_parts + [scaled_cot] + attn_weights,
        [
            pltpu.VMEM((model, 4 * inner), BF),
            pltpu.VMEM((frames, 3 * inner), BF),
            pltpu.VMEM((frames, inner), BF),
            pltpu.VMEM((frames, inner // heads), F32),
            pltpu.VMEM((frames, inner // heads), F32),
            pltpu.VMEM((frames, model), F32),
        ],
        flops=16 * frames * model * inner + 12 * frames * frames * inner,
        smem=3,
        far=2 if direct_rows else 0,
    )
    attn_normed, context, slopes = made[:3]
    attn_partial = made[3]
    upstream = scatter_frames(list(made[4:]))
    half = [shape((model // 2, 4 * inner), BF)] * 2
    attn_grads = call(
        attention_grads_kernel,
        half if direct_rows else [shape((model, 4 * inner), BF)],
        [me, attn_normed, scaled_cot, context, slopes],
        [pltpu.VMEM((model, inner), F32)],
        flops=8 * frames * model * inner,
        smem=1,
    )
    attn_terms, attn_sums = scatter_rows(attn_grads)
    (grad_mid_own,) = call(
        functools.partial(grad_mid_kernel, len(upstream), cot_scale),
        [shape((own, model), BF)],
        [attn_gain, mid_own, cot_own] + upstream,
    )
    grad_mid_parts = gather_frames(grad_mid_own)
    half = [shape((model // 2, 2 * hidden), BF)] * 2
    ffn_grads = call(
        functools.partial(ffn_grads_kernel, parts),
        half if direct_rows else [shape((model, 2 * hidden), BF)],
        [me, ffn_normed, ffn_pre, ffn_hidden, down_full] + grad_mid_parts,
        [pltpu.VMEM((frames, model), BF), pltpu.VMEM((model, hidden), F32)],
        flops=6 * frames * model * hidden,
        smem=1,
        after=attn_terms[1:3],
    )
    ffn_terms, passed = scatter_rows(ffn_grads, [attn_partial])
    if direct_frames:
        attn_sum = lax.all_to_all(passed[0], "ctx", 0, 0, tiled=True)
        attn_sum = add_terms([attn_sum[at * own : (at + 1) * own] for at in range(ctx)])
    else:
        attn_sum = lax.psum_scatter(passed[0], "ctx", scatter_dimension=0, tiled=True)
    block_out = (mid_own + attn_sum).astype(BF)[None]
    attn_total, ffn_total = add_terms(attn_terms), add_terms(ffn_terms)
    return (
        block_out,
        ffn_total[:, :hidden],
        ffn_total[:, hidden:],
        attn_total[:, :inner],
        attn_total[:, inner : 2 * inner],
        attn_total[:, 2 * inner : 3 * inner],
        attn_total[:, 3 * inner :],
    )


def solution(mesh):
    placed = (
        P("dp", "ctx", None),
        P("dp", None),
        P("dp", None),
        P(),
        P("dp", "ctx"),
        P("dp", "ctx"),
        P(),
        P("dp", "ctx"),
        P("dp", "ctx"),
        P("dp", "ctx"),
        P("dp", "ctx"),
        P("ctx", None),
        P("dp", "ctx", None),
    )
    return jax.shard_map(
        per_device,
        mesh=mesh,
        in_specs=placed,
        out_specs=(P("dp", "ctx", None),) + (P("dp", "ctx"),) * 6,
        check_vma=False,
    )
```

```python
import functools
import math

import jax
import jax.numpy as jnp
from jax import lax
from jax.experimental import pallas as pl
from jax.experimental.pallas import tpu as pltpu
from jax.sharding import PartitionSpec as P

SPAN = 64
BF = jnp.bfloat16
F32 = jnp.float32
MIB = 1024 * 1024


def exchange(values, axis, mask):
    size = lax.axis_size(axis)
    return lax.ppermute(values, axis, [(one, one ^ mask) for one in range(size)])


def call(body, outs, args, scratch=(), flops=0, smem=0, far=0, after=(), alone=False):
    count = len(args)
    specs = [pl.BlockSpec(memory_space=pltpu.SMEM)] * smem
    specs += [pl.BlockSpec(memory_space=pltpu.VMEM)] * (count - smem - far)
    specs += [pl.BlockSpec(memory_space=pl.ANY)] * (far + len(after))
    moved = sum(math.prod(one.shape) * one.dtype.itemsize for one in list(args) + list(outs))
    held = moved + sum(math.prod(one.shape) * jnp.dtype(one.dtype).itemsize for one in scratch)
    if far:
        scratch = [*scratch, pltpu.SemaphoreType.DMA((16,))]
    return pl.pallas_call(
        lambda *refs: body(*refs[:count], *refs[count + len(after) :]),
        out_shape=tuple(outs),
        in_specs=specs,
        out_specs=tuple(pl.BlockSpec(memory_space=pltpu.VMEM) for _ in outs),
        scratch_shapes=list(scratch),
        compiler_params=pltpu.CompilerParams(vmem_limit_bytes=60 * MIB if alone else min(held + 6 * MIB, 56 * MIB)),
        cost_estimate=pl.CostEstimate(flops=flops, bytes_accessed=moved, transcendentals=0),
    )(*args, *after)


def shape(dims, dtype):
    return jax.ShapeDtypeStruct(dims, dtype)


def dot(left, right, left_dim, right_dim):
    return lax.dot_general(
        left, right, (((left_dim,), (right_dim,)), ((), ())), preferred_element_type=F32
    )


def normalise(values):
    center = values - jnp.mean(values, axis=-1, keepdims=True)
    variance = jnp.mean(center * center, axis=-1, keepdims=True)
    inverse = lax.rsqrt(variance + 1e-05)
    return center * inverse, inverse


def start_copies(pairs, sems, first_sem=0):
    copies = []
    for at, (source, target) in enumerate(pairs):
        copies.append(pltpu.make_async_copy(source, target, sems.at[first_sem + at]))
        copies[-1].start()
    return copies


def wait_copies(copies):
    for one in copies:
        one.wait()


def collect(me_ref, pieces, ids, first_column, target, sems, first_sem=0):
    rows, width = target.shape
    rows = rows // len(ids)
    columns = slice(first_column, first_column + width)
    if len(ids) == 1:
        target[...] = pieces[0][:, columns]
        return []
    blocks = [(piece, at) for piece in pieces for at in range(0, piece.shape[0], rows)]
    pairs = []
    for (piece, at), mask in zip(blocks, ids):
        first = pl.multiple_of((me_ref[0] ^ mask) * rows, 16)
        source = piece.at[pl.ds(at, rows), pl.ds(first_column, width)]
        pairs.append((source, target.at[pl.ds(first, rows), :]))
    return start_copies(pairs, sems, first_sem)


def hand_out(me_ref, total, firsts, rows, outs, first_column):
    width = total.shape[1]
    columns = slice(first_column, first_column + width)
    if len(outs) == 1:
        outs[0][:, columns] = total[...].astype(BF)
        return
    blocks = [(out, at) for out in outs for at in range(0, out.shape[0], rows)]
    for (out, at), first in zip(blocks, firsts):
        block = total[pl.ds(pl.multiple_of(first * rows, 8), rows), :]
        out[at : at + rows, columns] = block.astype(BF)


def ffn_kernel(parts, ids, cot_scale, *refs):
    place_ref, me_ref, gain = refs[:3]
    both_parts = refs[3 : 3 + parts]
    direct = len(ids) > 1
    at = 3 + parts + (2 if direct else 1)
    weights, rest = refs[3 + parts : at], refs[at:]
    normed_out, pre_out, hidden_out, down, scaled = rest[:5]
    partials = rest[5 : 5 + parts]
    up = rest[5 + parts]
    sems = rest[-1]
    model, width = up.shape
    up_copies = collect(me_ref, weights, ids, 0, up, sems)
    down_copies = collect(me_ref, weights, ids, width, down, sems, 8)
    own = both_parts[0].shape[0]
    for index, (first, both) in enumerate(zip(places(place_ref, parts, own), both_parts)):
        normed = normalise(both[:, :model].astype(F32))[0] * gain[...].reshape(1, -1)
        normed_out[index * own : (index + 1) * own, :] = normed.astype(BF)
        cot = both[:, model:].astype(F32)
        scaled[pl.ds(first, own), :] = (cot * cot_scale).astype(BF)
    wait_copies(up_copies)
    pre = dot(normed_out[...], up[...], 1, 0)
    pre_out[...] = pre
    hidden_out[...] = (pre * jax.nn.sigmoid(pre)).astype(BF)
    wait_copies(down_copies)
    made = dot(hidden_out[...], down[...], 1, 1)
    for index, out in enumerate(partials):
        out[...] = made[index * own : (index + 1) * own].astype(BF)


def places(place_ref, parts, own):
    if parts == 1:
        return [0]
    return [pl.multiple_of((place_ref[0] ^ mask) * own, 16) for mask in range(parts)]


def mid_kernel(parts, *refs):
    gain, frames = refs[0], refs[1]
    pieces = refs[2 : 2 + parts]
    stacked = 4 if len(refs) > parts + 4 else 0
    weights = refs[2 + parts : 2 + parts + stacked]
    mid_out, normed_out = refs[2 + parts + stacked : 4 + parts + stacked]
    copies = []
    if stacked:
        near, sems = refs[-2:]
        copies = start_copies(row_pairs(weights, near), sems)
    total = pieces[0][...].astype(F32)
    for piece in pieces[1:]:
        total = total + piece[...].astype(F32)
    mid = frames[...].astype(F32) + 0.5 * total
    mid_out[...] = mid
    normed_out[...] = (normalise(mid)[0] * gain[...].reshape(1, -1)).astype(BF)
    wait_copies(copies)


def attention_kernel(parts, ids, window, *refs):
    place_ref, me_ref, bias = refs[:3]
    segments, spans = refs[3:5]
    normed_parts = refs[5 : 5 + parts]
    scaled = refs[5 + parts]
    at = 6 + parts + (2 if len(ids) > 1 else 1)
    weights_in, rest = refs[6 + parts : at], refs[at:]
    normed, context, slopes = rest[:3]
    attn_out, outs = rest[3], rest[4 : 4 + parts]
    weights, qkv, grad_context, key_total, value_total, total = rest[4 + parts : 10 + parts]
    copies = collect(me_ref, weights_in, ids, 0, weights, rest[-1])
    heads = bias.shape[0]
    frames = normed.shape[0]
    own = normed_parts[0].shape[0]
    inner = context.shape[1]
    width = inner // heads
    scale = width ** (-0.5)
    firsts = places(place_ref, parts, own)
    for first, piece in zip(firsts, normed_parts):
        normed[pl.ds(first, own), :] = piece[...]
    wait_copies(copies)
    qkv[...] = dot(normed[...], weights[:, : 3 * inner], 1, 0).astype(BF)
    grad_context[...] = dot(scaled[...], weights[:, 3 * inner :], 1, 0).astype(BF)
    seg_k, span_k = segments[...], spans[...]
    seg_q = jnp.transpose(jnp.broadcast_to(seg_k, (8, frames)))[:, :1]
    span_q = jnp.transpose(jnp.broadcast_to(span_k, (8, frames)))[:, :1]
    block = min(frames, 256)
    reach = min(window, (frames - 1) // SPAN)
    for head in range(heads):
        cols = slice(head * width, (head + 1) * width)
        key_cols = slice(inner + head * width, inner + (head + 1) * width)
        value_cols = slice(2 * inner + head * width, 2 * inner + (head + 1) * width)
        key = qkv[:, key_cols]
        value = qkv[:, value_cols]
        for first in range(0, frames, block):
            mine = slice(first, first + block)
            query = qkv[mine, cols]
            distance = span_q[mine, :] - span_k
            allowed = (seg_q[mine, :] == seg_k) & (distance >= 0) & (distance <= window)
            added = jnp.full((block, frames), bias[head, 0], F32)
            for far in range(1, reach + 1):
                added = jnp.where(distance == far, bias[head, far], added)
            scores = dot(query, key, 1, 1) * scale + added
            scores = jnp.where(allowed, scores, -1e30)
            expo = jnp.exp(scores - jnp.max(scores, axis=-1, keepdims=True))
            soft = expo / jnp.sum(expo, axis=-1, keepdims=True)
            low = soft.astype(BF)
            context[mine, cols] = dot(low, value, 1, 0).astype(BF)
            slope = grad_context[mine, cols]
            probs = dot(slope, value, 1, 1)
            probs = probs - jnp.sum(soft * probs, axis=-1, keepdims=True)
            grad = (soft * probs).astype(BF)
            slopes[mine, cols] = (dot(grad, key, 1, 0) * scale).astype(BF)
            key_slope = dot(grad, query, 0, 0)
            value_slope = dot(low, slope, 0, 0)
            if first > 0:
                key_slope = key_total[...] + key_slope
                value_slope = value_total[...] + value_slope
            if first + block < frames:
                key_total[...] = key_slope
                value_total[...] = value_slope
        slopes[:, key_cols] = (key_slope * scale).astype(BF)
        slopes[:, value_cols] = value_slope.astype(BF)
    total[...] = dot(slopes[...], weights[:, : 3 * inner], 1, 1)
    for first, out in zip(firsts, outs):
        out[...] = total[pl.ds(first, own), :].astype(BF)
    total[...] = dot(context[...], weights[:, 3 * inner :], 1, 1)
    attn_out[...] = total[...].astype(BF)


def attention_grads_kernel(*refs):
    me_ref, normed, scaled, context, slopes = refs[:5]
    outs, total = refs[5:-1], refs[-1]
    inner = context.shape[1]
    rows = total.shape[0] // 8
    firsts = [me_ref[0] ^ mask for mask in (0, 2, 4, 6, 1, 3, 5, 7)]
    for index in range(3):
        total[...] = dot(normed[...], slopes[:, index * inner : (index + 1) * inner], 0, 0)
        hand_out(me_ref, total, firsts, rows, outs, index * inner)
    total[...] = dot(scaled[...], context[...], 0, 0)
    hand_out(me_ref, total, firsts, rows, outs, 3 * inner)


def grad_mid_kernel(parts, cot_scale, *refs):
    gain, mid, cot = refs[:3]
    pieces = refs[3 : 3 + parts]
    out = refs[3 + parts]
    upstream = pieces[0][...].astype(F32)
    for piece in pieces[1:]:
        upstream = upstream + piece[...].astype(F32)
    normed, inverse = normalise(mid[...])
    scaled = upstream * gain[...].reshape(1, -1)
    first = jnp.mean(scaled, axis=-1, keepdims=True)
    second = jnp.mean(scaled * normed, axis=-1, keepdims=True)
    slope = inverse * (scaled - first - normed * second)
    low_cot = (cot[...].astype(F32) * cot_scale).astype(BF).astype(F32)
    out[...] = (low_cot + slope).astype(BF)


def ffn_grads_kernel(parts, *refs):
    me_ref, normed, pre, hidden, down = refs[:5]
    mids = refs[5 : 5 + parts]
    outs = refs[5 + parts : -2]
    grad_mid, total = refs[-2:]
    own = mids[0].shape[0]
    rows = total.shape[0] // 8
    firsts = [me_ref[0] ^ mask for mask in (0, 2, 4, 6, 1, 3, 5, 7)]
    for index, piece in enumerate(mids):
        grad_mid[index * own : (index + 1) * own, :] = piece[...]
    total[...] = 0.5 * dot(grad_mid[...], hidden[...], 0, 0)
    hand_out(me_ref, total, firsts, rows, outs, down.shape[1])
    sigma = jax.nn.sigmoid(pre[...])
    slope = sigma * (1.0 + pre[...] * (1.0 - sigma))
    grad_hidden = (0.5 * dot(grad_mid[...], down[...], 1, 0) * slope).astype(BF)
    total[...] = dot(normed[...], grad_hidden, 0, 0)
    hand_out(me_ref, total, firsts, rows, outs, 0)


def pair_sum_kernel(keep, came, *refs):
    passed = (len(refs) - 4) // 2
    rows = keep.shape[0] // 4
    for at, out in enumerate(refs[passed : passed + 4]):
        mine = slice(at * rows, (at + 1) * rows)
        out[...] = (keep[mine, :].astype(F32) + came[mine, :].astype(F32)).astype(BF)
    for one, out in zip(refs[:passed], refs[passed + 4 :]):
        out[...] = one[...]


def row_pairs(pieces, out):
    starts = [sum(one.shape[0] for one in pieces[:at]) for at in range(len(pieces))]
    return [(one, out.at[pl.ds(at, one.shape[0]), :]) for one, at in zip(pieces, starts)]


def column_pairs(pieces, out):
    starts = [sum(one.shape[1] for one in pieces[:at]) for at in range(len(pieces))]
    return [(one, out.at[:, pl.ds(at, one.shape[1])]) for one, at in zip(pieces, starts)]


def stack_kernel(*refs):
    wait_copies(start_copies(row_pairs(refs[:-2], refs[-2]), refs[-1]))


def pack_kernel(groups, *refs):
    outs, pairs, at = refs[sum(groups) : -1], [], 0
    for count, out in zip(groups, outs):
        pairs += column_pairs(refs[at : at + count], out)
        at += count
    wait_copies(start_copies(pairs, refs[-1]))


def stack(pieces, after=()):
    total = sum(one.shape[0] for one in pieces)
    out = shape((total, pieces[0].shape[1]), BF)
    return call(stack_kernel, [out], pieces, far=len(pieces), after=after)[0]


def pack(groups, after=(), alone=False):
    outs = [
        shape((group[0].shape[0], sum(one.shape[1] for one in group)), BF) for group in groups
    ]
    whole = all(one.shape[0] % 16 == 0 and one.shape[1] % 128 == 0 for group in groups for one in group)
    if not whole:
        return [jnp.concatenate(group, axis=1) for group in groups]
    pieces = [one for group in groups for one in group]
    body = functools.partial(pack_kernel, tuple(len(group) for group in groups))
    return call(body, outs, pieces, far=len(pieces), after=after, alone=alone)


def per_device(
    frames_in,
    segment_ids,
    span_ids,
    ffn_gain,
    w_up,
    w_down,
    attn_gain,
    w_query,
    w_key,
    w_value,
    w_out,
    offset_bias,
    cotangent,
):
    dp, ctx = lax.axis_size("dp"), lax.axis_size("ctx")
    own, model = frames_in.shape[1:]
    frames = own * ctx
    heads = offset_bias.shape[0]
    window = offset_bias.shape[1] - 1
    hidden, inner = w_up.shape[1], w_query.shape[1]
    rows = w_up.shape[0]
    direct_rows = dp == 8 and rows % 16 == 0
    direct_frames = ctx == 4 and own % 16 == 0
    ids = (0, 6, 4, 2, 1, 7, 5, 3) if direct_rows else (0,)
    parts = ctx if direct_frames else 1
    part_rows = frames // parts
    me = lax.axis_index("dp").astype(jnp.int32).reshape(1)
    place = lax.axis_index("ctx").astype(jnp.int32).reshape(1)
    cot_scale = 1.0 / math.sqrt(dp * frames)

    def gather_frames(values, relay=False):
        if not direct_frames:
            return [lax.all_gather(values, "ctx", axis=0, tiled=True)]
        parts = [values] + [exchange(values, "ctx", mask) for mask in (1, 2)]
        return parts + [exchange(*((parts[2], "ctx", 1) if relay else (values, "ctx", 3)))]

    def scatter_frames(pieces):
        if not direct_frames:
            return [lax.psum_scatter(pieces[0], "ctx", scatter_dimension=0, tiled=True)]
        return [pieces[0]] + [exchange(pieces[mask], "ctx", mask) for mask in (1, 2, 3)]

    def scatter_rows(pieces, passed=(), after=()):
        if not direct_rows:
            made = lax.psum_scatter(pieces[0], "dp", scatter_dimension=0, tiled=True)
            return [made], passed
        keep, send = pieces
        came = exchange(send, "dp", 1)
        outs = [shape((rows, keep.shape[1]), BF)] * 4 + [shape(one.shape, BF) for one in passed]
        sums = call(pair_sum_kernel, outs, [keep, came, *passed], after=after)
        terms = [sums[0]] + [exchange(sums[at], "dp", 2 * at) for at in (1, 2, 3)]
        return terms, sums[4:] if passed else sums[:1]

    def add_terms(terms):
        total = terms[0].astype(F32)
        for one in terms[1:]:
            total = total + one.astype(F32)
        return total

    frames_own, cot_own = frames_in[0], cotangent[0]
    both_own, ffn_rows = pack([[frames_own, cot_own], [w_up, w_down]], alone=True)
    both_parts = gather_frames(both_own, True)

    def gather_near(weight):
        return [weight] + [exchange(weight, "dp", mask) for mask in (6, 4, 2)]

    if direct_rows:
        ffn_near = stack(gather_near(ffn_rows), both_parts[1:])
        ffn_weights = [ffn_near, exchange(ffn_near, "dp", 1)]
        attn_pieces = gather_near(pack([[w_query, w_key, w_value, w_out]], [ffn_near])[0])
    else:
        ffn_weights = [lax.all_gather(ffn_rows, "dp", axis=0, tiled=True)]
        attn_weights = pack([[w_query, w_key, w_value, w_out]])[0]
        attn_weights = [lax.all_gather(attn_weights, "dp", axis=0, tiled=True)]
        attn_pieces = []

    made = call(
        functools.partial(ffn_kernel, parts, ids, cot_scale),
        [
            shape((frames, model), BF),
            shape((frames, hidden), F32),
            shape((frames, hidden), BF),
            shape((model, hidden), BF),
            shape((frames, model), BF),
        ]
        + [shape((part_rows, model), BF)] * parts,
        [place, me, ffn_gain] + both_parts + ffn_weights,
        [pltpu.VMEM((model, hidden), BF)],
        flops=4 * frames * model * hidden,
        smem=2,
        far=2 if direct_rows else 0,
    )
    ffn_normed, ffn_pre, ffn_hidden, down_full, scaled_cot = made[:5]
    summed = scatter_frames(list(made[5:]))
    near = [shape((model // 2, 4 * inner), BF)] if direct_rows else []
    mid_own, normed_own, *near = call(
        functools.partial(mid_kernel, len(summed)),
        [shape((own, model), F32), shape((own, model), BF)] + near,
        [attn_gain, frames_own] + summed + attn_pieces,
        far=len(attn_pieces),
    )
    normed_parts = gather_frames(normed_own)
    if direct_rows:
        attn_weights = [near[0], exchange(near[0], "dp", 1)]
    made = call(
        functools.partial(attention_kernel, parts, ids, window),
        [
            shape((frames, model), BF),
            shape((frames, inner), BF),
            shape((frames, 3 * inner), BF),
            shape((frames, model), BF),
        ]
        + [shape((part_rows, model), BF)] * parts,
        [place, me, offset_bias, segment_ids, span_ids] + normed_parts + [scaled_cot] + attn_weights,
        [
            pltpu.VMEM((model, 4 * inner), BF),
            pltpu.VMEM((frames, 3 * inner), BF),
            pltpu.VMEM((frames, inner), BF),
            pltpu.VMEM((frames, inner // heads), F32),
            pltpu.VMEM((frames, inner // heads), F32),
            pltpu.VMEM((frames, model), F32),
        ],
        flops=16 * frames * model * inner + 12 * frames * frames * inner,
        smem=3,
        far=2 if direct_rows else 0,
    )
    attn_normed, context, slopes = made[:3]
    attn_partial = made[3]
    upstream = scatter_frames(list(made[4:]))
    half = [shape((model // 2, 4 * inner), BF)] * 2
    attn_grads = call(
        attention_grads_kernel,
        half if direct_rows else [shape((model, 4 * inner), BF)],
        [me, attn_normed, scaled_cot, context, slopes],
        [pltpu.VMEM((model, inner), F32)],
        flops=8 * frames * model * inner,
        smem=1,
    )
    attn_terms, attn_sums = scatter_rows(attn_grads, after=upstream[1:])
    (grad_mid_own,) = call(
        functools.partial(grad_mid_kernel, len(upstream), cot_scale),
        [shape((own, model), BF)],
        [attn_gain, mid_own, cot_own] + upstream,
    )
    grad_mid_parts = gather_frames(grad_mid_own)
    half = [shape((model // 2, 2 * hidden), BF)] * 2
    ffn_grads = call(
        functools.partial(ffn_grads_kernel, parts),
        half if direct_rows else [shape((model, 2 * hidden), BF)],
        [me, ffn_normed, ffn_pre, ffn_hidden, down_full] + grad_mid_parts,
        [pltpu.VMEM((frames, model), BF), pltpu.VMEM((model, hidden), F32)],
        flops=6 * frames * model * hidden,
        smem=1,
        after=attn_terms[1:3],
    )
    ffn_terms, passed = scatter_rows(ffn_grads, [attn_partial])
    if direct_frames:
        attn_sum = lax.all_to_all(passed[0], "ctx", 0, 0, tiled=True)
        attn_sum = add_terms([attn_sum[at * own : (at + 1) * own] for at in range(ctx)])
    else:
        attn_sum = lax.psum_scatter(passed[0], "ctx", scatter_dimension=0, tiled=True)
    block_out = (mid_own + attn_sum).astype(BF)[None]
    attn_total, ffn_total = add_terms(attn_terms), add_terms(ffn_terms)
    return (
        block_out,
        ffn_total[:, :hidden],
        ffn_total[:, hidden:],
        attn_total[:, :inner],
        attn_total[:, inner : 2 * inner],
        attn_total[:, 2 * inner : 3 * inner],
        attn_total[:, 3 * inner :],
    )


def solution(mesh):
    placed = (
        P("dp", "ctx", None),
        P("dp", None),
        P("dp", None),
        P(),
        P("dp", "ctx"),
        P("dp", "ctx"),
        P(),
        P("dp", "ctx"),
        P("dp", "ctx"),
        P("dp", "ctx"),
        P("dp", "ctx"),
        P("ctx", None),
        P("dp", "ctx", None),
    )
    return jax.shard_map(
        per_device,
        mesh=mesh,
        in_specs=placed,
        out_specs=(P("dp", "ctx", None),) + (P("dp", "ctx"),) * 6,
        check_vma=False,
    )
```

```python
import functools
import math

import jax
import jax.numpy as jnp
from jax import lax
from jax.experimental import pallas as pl
from jax.experimental.pallas import tpu as pltpu
from jax.sharding import PartitionSpec as P

SPAN = 64
BF = jnp.bfloat16
F32 = jnp.float32
MIB = 1024 * 1024


def exchange(values, axis, mask):
    size = lax.axis_size(axis)
    return lax.ppermute(values, axis, [(one, one ^ mask) for one in range(size)])


def call(body, outs, args, scratch=(), flops=0, smem=0, far=0, after=(), alone=False):
    count = len(args)
    specs = [pl.BlockSpec(memory_space=pltpu.SMEM)] * smem
    specs += [pl.BlockSpec(memory_space=pltpu.VMEM)] * (count - smem - far)
    specs += [pl.BlockSpec(memory_space=pl.ANY)] * (far + len(after))
    moved = sum(math.prod(one.shape) * one.dtype.itemsize for one in list(args) + list(outs))
    held = moved + sum(math.prod(one.shape) * jnp.dtype(one.dtype).itemsize for one in scratch)
    if far:
        scratch = [*scratch, pltpu.SemaphoreType.DMA((16,))]
    return pl.pallas_call(
        lambda *refs: body(*refs[:count], *refs[count + len(after) :]),
        out_shape=tuple(outs),
        in_specs=specs,
        out_specs=tuple(pl.BlockSpec(memory_space=pltpu.VMEM) for _ in outs),
        scratch_shapes=list(scratch),
        compiler_params=pltpu.CompilerParams(vmem_limit_bytes=60 * MIB if alone else min(held + 6 * MIB, 56 * MIB)),
        cost_estimate=pl.CostEstimate(flops=flops, bytes_accessed=moved, transcendentals=0),
    )(*args, *after)


def shape(dims, dtype):
    return jax.ShapeDtypeStruct(dims, dtype)


def dot(left, right, left_dim, right_dim):
    return lax.dot_general(
        left, right, (((left_dim,), (right_dim,)), ((), ())), preferred_element_type=F32
    )


def normalise(values):
    center = values - jnp.mean(values, axis=-1, keepdims=True)
    variance = jnp.mean(center * center, axis=-1, keepdims=True)
    inverse = lax.rsqrt(variance + 1e-05)
    return center * inverse, inverse


def start_copies(pairs, sems, first_sem=0):
    copies = []
    for at, (source, target) in enumerate(pairs):
        copies.append(pltpu.make_async_copy(source, target, sems.at[first_sem + at]))
        copies[-1].start()
    return copies


def wait_copies(copies):
    for one in copies:
        one.wait()


def collect(me_ref, pieces, ids, first_column, target, sems, first_sem=0):
    rows, width = target.shape
    rows = rows // len(ids)
    columns = slice(first_column, first_column + width)
    if len(ids) == 1:
        target[...] = pieces[0][:, columns]
        return []
    blocks = [(piece, at) for piece in pieces for at in range(0, piece.shape[0], rows)]
    pairs = []
    for (piece, at), mask in zip(blocks, ids):
        first = pl.multiple_of((me_ref[0] ^ mask) * rows, 16)
        source = piece.at[pl.ds(at, rows), pl.ds(first_column, width)]
        pairs.append((source, target.at[pl.ds(first, rows), :]))
    return start_copies(pairs, sems, first_sem)


def hand_out(me_ref, total, firsts, rows, outs, first_column):
    width = total.shape[1]
    columns = slice(first_column, first_column + width)
    if len(outs) == 1:
        outs[0][:, columns] = total[...].astype(BF)
        return
    blocks = [(out, at) for out in outs for at in range(0, out.shape[0], rows)]
    for (out, at), first in zip(blocks, firsts):
        block = total[pl.ds(pl.multiple_of(first * rows, 8), rows), :]
        out[at : at + rows, columns] = block.astype(BF)


def ffn_kernel(parts, ids, cot_scale, *refs):
    place_ref, me_ref, gain = refs[:3]
    both_parts = refs[3 : 3 + parts]
    direct = len(ids) > 1
    at = 3 + parts + (2 if direct else 1)
    weights, rest = refs[3 + parts : at], refs[at:]
    normed_out, pre_out, hidden_out, down, scaled = rest[:5]
    partials = rest[5 : 5 + parts]
    up = rest[5 + parts]
    sems = rest[-1]
    model, width = up.shape
    up_copies = collect(me_ref, weights, ids, 0, up, sems)
    down_copies = collect(me_ref, weights, ids, width, down, sems, 8)
    own = both_parts[0].shape[0]
    for index, (first, both) in enumerate(zip(places(place_ref, parts, own), both_parts)):
        normed = normalise(both[:, :model].astype(F32))[0] * gain[...].reshape(1, -1)
        normed_out[index * own : (index + 1) * own, :] = normed.astype(BF)
        cot = both[:, model:].astype(F32)
        scaled[pl.ds(first, own), :] = (cot * cot_scale).astype(BF)
    wait_copies(up_copies)
    pre = dot(normed_out[...], up[...], 1, 0)
    pre_out[...] = pre
    hidden_out[...] = (pre * jax.nn.sigmoid(pre)).astype(BF)
    wait_copies(down_copies)
    made = dot(hidden_out[...], down[...], 1, 1)
    for index, out in enumerate(partials):
        out[...] = made[index * own : (index + 1) * own].astype(BF)


def places(place_ref, parts, own):
    if parts == 1:
        return [0]
    return [pl.multiple_of((place_ref[0] ^ mask) * own, 16) for mask in range(parts)]


def mid_kernel(parts, *refs):
    gain, frames = refs[0], refs[1]
    pieces = refs[2 : 2 + parts]
    stacked = 4 if len(refs) > parts + 4 else 0
    weights = refs[2 + parts : 2 + parts + stacked]
    mid_out, normed_out = refs[2 + parts + stacked : 4 + parts + stacked]
    copies = []
    if stacked:
        near, sems = refs[-2:]
        copies = start_copies(row_pairs(weights, near), sems)
    total = pieces[0][...].astype(F32)
    for piece in pieces[1:]:
        total = total + piece[...].astype(F32)
    mid = frames[...].astype(F32) + 0.5 * total
    mid_out[...] = mid
    normed_out[...] = (normalise(mid)[0] * gain[...].reshape(1, -1)).astype(BF)
    wait_copies(copies)


def collect_kernel(ids, me_ref, near, far, out, sems):
    wait_copies(collect(me_ref, [near, far], ids, 0, out, sems))


def attention_kernel(parts, window, *refs):
    place_ref, bias = refs[:2]
    segments, spans = refs[2:4]
    normed_parts = refs[4 : 4 + parts]
    scaled, weights = refs[4 + parts : 6 + parts]
    rest = refs[6 + parts :]
    normed, context, slopes = rest[:3]
    outs = rest[3 : 3 + parts]
    halves = 1 if parts == 1 else 2
    attn_outs = rest[3 + parts : 3 + parts + halves]
    qkv, grad_context, key_total, value_total, total = rest[3 + parts + halves :]
    heads = bias.shape[0]
    frames = normed.shape[0]
    own = normed_parts[0].shape[0]
    inner = context.shape[1]
    width = inner // heads
    scale = width ** (-0.5)
    firsts = places(place_ref, parts, own)
    for first, piece in zip(firsts, normed_parts):
        normed[pl.ds(first, own), :] = piece[...]
    qkv[...] = dot(normed[...], weights[:, : 3 * inner], 1, 0).astype(BF)
    grad_context[...] = dot(scaled[...], weights[:, 3 * inner :], 1, 0).astype(BF)
    seg_k, span_k = segments[...], spans[...]
    seg_q = jnp.transpose(jnp.broadcast_to(seg_k, (8, frames)))[:, :1]
    span_q = jnp.transpose(jnp.broadcast_to(span_k, (8, frames)))[:, :1]
    block = min(frames, 256)
    reach = min(window, (frames - 1) // SPAN)
    for head in range(heads):
        cols = slice(head * width, (head + 1) * width)
        key_cols = slice(inner + head * width, inner + (head + 1) * width)
        value_cols = slice(2 * inner + head * width, 2 * inner + (head + 1) * width)
        key = qkv[:, key_cols]
        value = qkv[:, value_cols]
        for first in range(0, frames, block):
            mine = slice(first, first + block)
            query = qkv[mine, cols]
            distance = span_q[mine, :] - span_k
            allowed = (seg_q[mine, :] == seg_k) & (distance >= 0) & (distance <= window)
            added = jnp.full((block, frames), bias[head, 0], F32)
            for far in range(1, reach + 1):
                added = jnp.where(distance == far, bias[head, far], added)
            scores = dot(query, key, 1, 1) * scale + added
            scores = jnp.where(allowed, scores, -1e30)
            expo = jnp.exp(scores - jnp.max(scores, axis=-1, keepdims=True))
            soft = expo / jnp.sum(expo, axis=-1, keepdims=True)
            low = soft.astype(BF)
            context[mine, cols] = dot(low, value, 1, 0).astype(BF)
            slope = grad_context[mine, cols]
            probs = dot(slope, value, 1, 1)
            probs = probs - jnp.sum(soft * probs, axis=-1, keepdims=True)
            grad = (soft * probs).astype(BF)
            slopes[mine, cols] = (dot(grad, key, 1, 0) * scale).astype(BF)
            key_slope = dot(grad, query, 0, 0)
            value_slope = dot(low, slope, 0, 0)
            if first > 0:
                key_slope = key_total[...] + key_slope
                value_slope = value_total[...] + value_slope
            if first + block < frames:
                key_total[...] = key_slope
                value_total[...] = value_slope
        slopes[:, key_cols] = (key_slope * scale).astype(BF)
        slopes[:, value_cols] = value_slope.astype(BF)
    total[...] = dot(slopes[...], weights[:, : 3 * inner], 1, 1)
    for first, out in zip(firsts, outs):
        out[...] = total[pl.ds(first, own), :].astype(BF)
    total[...] = dot(context[...], weights[:, 3 * inner :], 1, 1)
    if parts == 1:
        attn_outs[0][...] = total[...].astype(BF)
        return
    for index, out in enumerate(attn_outs):
        for at, first in enumerate((firsts[index], firsts[index + 2])):
            out[at * own : (at + 1) * own, :] = total[pl.ds(first, own), :].astype(BF)


def attention_grads_kernel(*refs):
    me_ref, normed, scaled, context, slopes = refs[:5]
    outs, total = refs[5:-1], refs[-1]
    inner = context.shape[1]
    rows = total.shape[0] // 8
    firsts = [me_ref[0] ^ mask for mask in (0, 2, 4, 6, 1, 3, 5, 7)]
    for index in range(3):
        total[...] = dot(normed[...], slopes[:, index * inner : (index + 1) * inner], 0, 0)
        hand_out(me_ref, total, firsts, rows, outs, index * inner)
    total[...] = dot(scaled[...], context[...], 0, 0)
    hand_out(me_ref, total, firsts, rows, outs, 3 * inner)


def grad_mid_kernel(parts, cot_scale, *refs):
    gain, mid, cot = refs[:3]
    pieces = refs[3 : 3 + parts]
    out = refs[3 + parts]
    upstream = pieces[0][...].astype(F32)
    for piece in pieces[1:]:
        upstream = upstream + piece[...].astype(F32)
    normed, inverse = normalise(mid[...])
    scaled = upstream * gain[...].reshape(1, -1)
    first = jnp.mean(scaled, axis=-1, keepdims=True)
    second = jnp.mean(scaled * normed, axis=-1, keepdims=True)
    slope = inverse * (scaled - first - normed * second)
    low_cot = (cot[...].astype(F32) * cot_scale).astype(BF).astype(F32)
    out[...] = (low_cot + slope).astype(BF)


def ffn_grads_kernel(parts, *refs):
    me_ref, normed, pre, hidden, down = refs[:5]
    mids = refs[5 : 5 + parts]
    outs = refs[5 + parts : -2]
    grad_mid, total = refs[-2:]
    own = mids[0].shape[0]
    rows = total.shape[0] // 8
    firsts = [me_ref[0] ^ mask for mask in (0, 2, 4, 6, 1, 3, 5, 7)]
    for index, piece in enumerate(mids):
        grad_mid[index * own : (index + 1) * own, :] = piece[...]
    total[...] = 0.5 * dot(grad_mid[...], hidden[...], 0, 0)
    hand_out(me_ref, total, firsts, rows, outs, down.shape[1])
    sigma = jax.nn.sigmoid(pre[...])
    slope = sigma * (1.0 + pre[...] * (1.0 - sigma))
    grad_hidden = (0.5 * dot(grad_mid[...], down[...], 1, 0) * slope).astype(BF)
    total[...] = dot(normed[...], grad_hidden, 0, 0)
    hand_out(me_ref, total, firsts, rows, outs, 0)


def pair_sum_kernel(keep, came, *refs):
    passed = (len(refs) - 4) // 2
    rows = keep.shape[0] // 4
    for at, out in enumerate(refs[passed : passed + 4]):
        mine = slice(at * rows, (at + 1) * rows)
        out[...] = (keep[mine, :].astype(F32) + came[mine, :].astype(F32)).astype(BF)
    for one, out in zip(refs[:passed], refs[passed + 4 :]):
        out[...] = one[...]


def half_sum_kernel(keep, came, mine, other):
    own = mine.shape[0]
    mine[...] = keep[:own, :].astype(F32) + came[:own, :].astype(F32)
    other[...] = (keep[own:, :].astype(F32) + came[own:, :].astype(F32)).astype(BF)


def row_pairs(pieces, out):
    starts = [sum(one.shape[0] for one in pieces[:at]) for at in range(len(pieces))]
    return [(one, out.at[pl.ds(at, one.shape[0]), :]) for one, at in zip(pieces, starts)]


def column_pairs(pieces, out):
    starts = [sum(one.shape[1] for one in pieces[:at]) for at in range(len(pieces))]
    return [(one, out.at[:, pl.ds(at, one.shape[1])]) for one, at in zip(pieces, starts)]


def stack_kernel(*refs):
    wait_copies(start_copies(row_pairs(refs[:-2], refs[-2]), refs[-1]))


def pack_kernel(groups, *refs):
    outs, pairs, at = refs[sum(groups) : -1], [], 0
    for count, out in zip(groups, outs):
        pairs += column_pairs(refs[at : at + count], out)
        at += count
    wait_copies(start_copies(pairs, refs[-1]))


def stack(pieces, after=()):
    total = sum(one.shape[0] for one in pieces)
    out = shape((total, pieces[0].shape[1]), BF)
    return call(stack_kernel, [out], pieces, far=len(pieces), after=after)[0]


def pack(groups, after=(), alone=False):
    outs = [
        shape((group[0].shape[0], sum(one.shape[1] for one in group)), BF) for group in groups
    ]
    whole = all(one.shape[0] % 16 == 0 and one.shape[1] % 128 == 0 for group in groups for one in group)
    if not whole:
        return [jnp.concatenate(group, axis=1) for group in groups]
    pieces = [one for group in groups for one in group]
    body = functools.partial(pack_kernel, tuple(len(group) for group in groups))
    return call(body, outs, pieces, far=len(pieces), after=after, alone=alone)


def per_device(
    frames_in,
    segment_ids,
    span_ids,
    ffn_gain,
    w_up,
    w_down,
    attn_gain,
    w_query,
    w_key,
    w_value,
    w_out,
    offset_bias,
    cotangent,
):
    dp, ctx = lax.axis_size("dp"), lax.axis_size("ctx")
    own, model = frames_in.shape[1:]
    frames = own * ctx
    heads = offset_bias.shape[0]
    window = offset_bias.shape[1] - 1
    hidden, inner = w_up.shape[1], w_query.shape[1]
    rows = w_up.shape[0]
    direct_rows = dp == 8 and rows % 16 == 0
    direct_frames = ctx == 4 and own % 16 == 0
    ids = (0, 6, 4, 2, 1, 7, 5, 3) if direct_rows else (0,)
    parts = ctx if direct_frames else 1
    part_rows = frames // parts
    me = lax.axis_index("dp").astype(jnp.int32).reshape(1)
    place = lax.axis_index("ctx").astype(jnp.int32).reshape(1)
    cot_scale = 1.0 / math.sqrt(dp * frames)

    def gather_frames(values, relay=False):
        if not direct_frames:
            return [lax.all_gather(values, "ctx", axis=0, tiled=True)]
        if relay:
            second, first = exchange(values, "ctx", 2), exchange(values, "ctx", 1)
            return [values, first, second, exchange(second, "ctx", 1)]
        return [values] + [exchange(values, "ctx", mask) for mask in (3, 2, 1)][::-1]

    def scatter_frames(pieces):
        if not direct_frames:
            return [lax.psum_scatter(pieces[0], "ctx", scatter_dimension=0, tiled=True)]
        return [pieces[0]] + [exchange(pieces[mask], "ctx", mask) for mask in (3, 2, 1)][::-1]

    def scatter_rows(pieces, passed=(), after=()):
        if not direct_rows:
            made = lax.psum_scatter(pieces[0], "dp", scatter_dimension=0, tiled=True)
            return [made], passed
        keep, send = pieces
        came = exchange(send, "dp", 1)
        outs = [shape((rows, keep.shape[1]), BF)] * 4 + [shape(one.shape, BF) for one in passed]
        sums = call(pair_sum_kernel, outs, [keep, came, *passed], after=after)
        terms = [sums[0]] + [exchange(sums[at], "dp", 2 * at) for at in (1, 2, 3)]
        return terms, sums[4:] if passed else sums[:1]

    def add_terms(terms):
        total = terms[0].astype(F32)
        for one in terms[1:]:
            total = total + one.astype(F32)
        return total

    frames_own, cot_own = frames_in[0], cotangent[0]
    both_own, ffn_rows = pack([[frames_own, cot_own], [w_up, w_down]], alone=True)
    both_parts = gather_frames(both_own, True)

    def gather_near(weight):
        return [weight] + [exchange(weight, "dp", mask) for mask in (6, 4, 2)]

    if direct_rows:
        ffn_near = stack(gather_near(ffn_rows), both_parts[1:])
        ffn_weights = [ffn_near, exchange(ffn_near, "dp", 1)]
        attn_pieces = gather_near(pack([[w_query, w_key, w_value, w_out]], [ffn_near])[0])
    else:
        ffn_weights = [lax.all_gather(ffn_rows, "dp", axis=0, tiled=True)]
        attn_weights = pack([[w_query, w_key, w_value, w_out]])[0]
        attn_weights = [lax.all_gather(attn_weights, "dp", axis=0, tiled=True)]
        attn_pieces = []

    made = call(
        functools.partial(ffn_kernel, parts, ids, cot_scale),
        [
            shape((frames, model), BF),
            shape((frames, hidden), F32),
            shape((frames, hidden), BF),
            shape((model, hidden), BF),
            shape((frames, model), BF),
        ]
        + [shape((part_rows, model), BF)] * parts,
        [place, me, ffn_gain] + both_parts + ffn_weights,
        [pltpu.VMEM((model, hidden), BF)],
        flops=4 * frames * model * hidden,
        smem=2,
        far=2 if direct_rows else 0,
    )
    ffn_normed, ffn_pre, ffn_hidden, down_full, scaled_cot = made[:5]
    summed = scatter_frames(list(made[5:]))
    near = [shape((model // 2, 4 * inner), BF)] if direct_rows else []
    mid_own, normed_own, *near = call(
        functools.partial(mid_kernel, len(summed)),
        [shape((own, model), F32), shape((own, model), BF)] + near,
        [attn_gain, frames_own] + summed + attn_pieces,
        far=len(attn_pieces),
    )
    normed_parts = gather_frames(normed_own)
    if direct_rows:
        attn_weights = call(
            functools.partial(collect_kernel, ids),
            [shape((model, 4 * inner), BF)],
            [me, near[0], exchange(near[0], "dp", 1)],
            smem=1,
            far=2,
        )
    made = call(
        functools.partial(attention_kernel, parts, window),
        [
            shape((frames, model), BF),
            shape((frames, inner), BF),
            shape((frames, 3 * inner), BF),
        ]
        + [shape((part_rows, model), BF)] * parts
        + [shape((frames // 2, model), BF)] * 2 * (parts > 1)
        + [shape((frames, model), BF)] * (parts == 1),
        [place, offset_bias, segment_ids, span_ids, *normed_parts, scaled_cot, *attn_weights],
        [
            pltpu.VMEM((frames, 3 * inner), BF),
            pltpu.VMEM((frames, inner), BF),
            pltpu.VMEM((frames, inner // heads), F32),
            pltpu.VMEM((frames, inner // heads), F32),
            pltpu.VMEM((frames, model), F32),
        ],
        flops=16 * frames * model * inner + 12 * frames * frames * inner,
        smem=2,
    )
    attn_normed, context, slopes = made[:3]
    attn_partials = made[3 + parts :]
    upstream = scatter_frames(list(made[3 : 3 + parts]))
    half = [shape((model // 2, 4 * inner), BF)] * 2
    attn_grads = call(
        attention_grads_kernel,
        half if direct_rows else [shape((model, 4 * inner), BF)],
        [me, attn_normed, scaled_cot, context, slopes],
        [pltpu.VMEM((model, inner), F32)],
        flops=8 * frames * model * inner,
        smem=1,
    )
    attn_terms, attn_sums = scatter_rows(attn_grads, after=upstream[1:])
    (grad_mid_own,) = call(
        functools.partial(grad_mid_kernel, len(upstream), cot_scale),
        [shape((own, model), BF)],
        [attn_gain, mid_own, cot_own] + upstream,
    )
    grad_mid_parts = gather_frames(grad_mid_own)
    half = [shape((model // 2, 2 * hidden), BF)] * 2
    ffn_grads = call(
        functools.partial(ffn_grads_kernel, parts),
        half if direct_rows else [shape((model, 2 * hidden), BF)],
        [me, ffn_normed, ffn_pre, ffn_hidden, down_full] + grad_mid_parts,
        [pltpu.VMEM((frames, model), BF), pltpu.VMEM((model, hidden), F32)],
        flops=6 * frames * model * hidden,
        smem=1,
        after=attn_terms[1:3],
    )
    ffn_terms, passed = scatter_rows(ffn_grads, list(attn_partials[1:]))
    if direct_frames:
        keep, send = attn_partials[0], passed[0]
        attn_own, attn_far = call(
            half_sum_kernel,
            [shape((own, model), F32), shape((own, model), BF)],
            [keep, exchange(send, "ctx", 1)],
        )
        attn_sum = attn_own + exchange(attn_far, "ctx", 2).astype(F32)
    else:
        attn_sum = lax.psum_scatter(attn_partials[0], "ctx", scatter_dimension=0, tiled=True)
    block_out = (mid_own + attn_sum).astype(BF)[None]
    attn_total, ffn_total = add_terms(attn_terms), add_terms(ffn_terms)
    return (
        block_out,
        ffn_total[:, :hidden],
        ffn_total[:, hidden:],
        attn_total[:, :inner],
        attn_total[:, inner : 2 * inner],
        attn_total[:, 2 * inner : 3 * inner],
        attn_total[:, 3 * inner :],
    )


def solution(mesh):
    placed = (
        P("dp", "ctx", None),
        P("dp", None),
        P("dp", None),
        P(),
        P("dp", "ctx"),
        P("dp", "ctx"),
        P(),
        P("dp", "ctx"),
        P("dp", "ctx"),
        P("dp", "ctx"),
        P("dp", "ctx"),
        P("ctx", None),
        P("dp", "ctx", None),
    )
    return jax.shard_map(
        per_device,
        mesh=mesh,
        in_specs=placed,
        out_specs=(P("dp", "ctx", None),) + (P("dp", "ctx"),) * 6,
        check_vma=False,
    )
```

```python
import functools
import math

import jax
import jax.numpy as jnp
from jax import lax
from jax.experimental import pallas as pl
from jax.experimental.pallas import tpu as pltpu
from jax.sharding import PartitionSpec as P

SPAN = 64
BF = jnp.bfloat16
F32 = jnp.float32
MIB = 1024 * 1024


def exchange(values, axis, mask):
    size = lax.axis_size(axis)
    return lax.ppermute(values, axis, [(one, one ^ mask) for one in range(size)])


def call(body, outs, args, scratch=(), flops=0, smem=0, far=0, after=(), alone=False):
    count = len(args)
    specs = [pl.BlockSpec(memory_space=pltpu.SMEM)] * smem
    specs += [pl.BlockSpec(memory_space=pltpu.VMEM)] * (count - smem - far)
    specs += [pl.BlockSpec(memory_space=pl.ANY)] * (far + len(after))
    moved = sum(math.prod(one.shape) * one.dtype.itemsize for one in list(args) + list(outs))
    held = moved + sum(math.prod(one.shape) * jnp.dtype(one.dtype).itemsize for one in scratch)
    if far:
        scratch = [*scratch, pltpu.SemaphoreType.DMA((16,))]
    return pl.pallas_call(
        lambda *refs: body(*refs[:count], *refs[count + len(after) :]),
        out_shape=tuple(outs),
        in_specs=specs,
        out_specs=tuple(pl.BlockSpec(memory_space=pltpu.VMEM) for _ in outs),
        scratch_shapes=list(scratch),
        compiler_params=pltpu.CompilerParams(vmem_limit_bytes=60 * MIB if alone else min(held + 6 * MIB, 56 * MIB)),
        cost_estimate=pl.CostEstimate(flops=flops, bytes_accessed=moved, transcendentals=0),
    )(*args, *after)


def shape(dims, dtype):
    return jax.ShapeDtypeStruct(dims, dtype)


def dot(left, right, left_dim, right_dim):
    return lax.dot_general(
        left, right, (((left_dim,), (right_dim,)), ((), ())), preferred_element_type=F32
    )


def normalise(values):
    center = values - jnp.mean(values, axis=-1, keepdims=True)
    variance = jnp.mean(center * center, axis=-1, keepdims=True)
    inverse = lax.rsqrt(variance + 1e-05)
    return center * inverse, inverse


def start_copies(pairs, sems, first_sem=0):
    copies = []
    for at, (source, target) in enumerate(pairs):
        copies.append(pltpu.make_async_copy(source, target, sems.at[first_sem + at]))
        copies[-1].start()
    return copies


def wait_copies(copies):
    for one in copies:
        one.wait()


def collect(me_ref, pieces, ids, first_column, target, sems, first_sem=0):
    rows, width = target.shape
    rows = rows // len(ids)
    columns = slice(first_column, first_column + width)
    if len(ids) == 1:
        target[...] = pieces[0][:, columns]
        return []
    blocks = [(piece, at) for piece in pieces for at in range(0, piece.shape[0], rows)]
    pairs = []
    for (piece, at), mask in zip(blocks, ids):
        first = pl.multiple_of((me_ref[0] ^ mask) * rows, 16)
        source = piece.at[pl.ds(at, rows), pl.ds(first_column, width)]
        pairs.append((source, target.at[pl.ds(first, rows), :]))
    return start_copies(pairs, sems, first_sem)


def hand_out(me_ref, total, firsts, rows, outs, first_column):
    width = total.shape[1]
    columns = slice(first_column, first_column + width)
    if len(outs) == 1:
        outs[0][:, columns] = total[...].astype(BF)
        return
    blocks = [(out, at) for out in outs for at in range(0, out.shape[0], rows)]
    for (out, at), first in zip(blocks, firsts):
        block = total[pl.ds(pl.multiple_of(first * rows, 8), rows), :]
        out[at : at + rows, columns] = block.astype(BF)


def prepare_kernel(parts, cot_scale, *refs):
    place_ref, gain = refs[:2]
    both_parts = refs[2 : 2 + parts]
    normed_out, scaled = refs[2 + parts :]
    own, model = both_parts[0].shape[0], normed_out.shape[1]
    for index, (first, both) in enumerate(zip(places(place_ref, parts, own), both_parts)):
        normed = normalise(both[:, :model].astype(F32))[0] * gain[...].reshape(1, -1)
        normed_out[index * own : (index + 1) * own, :] = normed.astype(BF)
        cot = both[:, model:].astype(F32)
        scaled[pl.ds(first, own), :] = (cot * cot_scale).astype(BF)


def ffn_kernel(parts, ids, *refs):
    me_ref, normed = refs[:2]
    at = 3 if len(ids) == 1 else 4
    weights, rest = refs[2:at], refs[at:]
    pre_out, hidden_out, down = rest[:3]
    partials = rest[3 : 3 + parts]
    up, sems = rest[3 + parts], rest[-1]
    width = up.shape[1]
    up_copies = collect(me_ref, weights, ids, 0, up, sems)
    down_copies = collect(me_ref, weights, ids, width, down, sems, 8)
    own = partials[0].shape[0]
    wait_copies(up_copies)
    pre = dot(normed[...], up[...], 1, 0)
    pre_out[...] = pre
    hidden_out[...] = (pre * jax.nn.sigmoid(pre)).astype(BF)
    wait_copies(down_copies)
    made = dot(hidden_out[...], down[...], 1, 1)
    for index, out in enumerate(partials):
        out[...] = made[index * own : (index + 1) * own].astype(BF)


def places(place_ref, parts, own):
    if parts == 1:
        return [0]
    return [pl.multiple_of((place_ref[0] ^ mask) * own, 16) for mask in range(parts)]


def mid_kernel(parts, *refs):
    gain, frames = refs[0], refs[1]
    pieces = refs[2 : 2 + parts]
    stacked = 4 if len(refs) > parts + 4 else 0
    weights = refs[2 + parts : 2 + parts + stacked]
    mid_out, normed_out = refs[2 + parts + stacked : 4 + parts + stacked]
    copies = []
    if stacked:
        near, sems = refs[-2:]
        copies = start_copies(row_pairs(weights, near), sems)
    total = pieces[0][...].astype(F32)
    for piece in pieces[1:]:
        total = total + piece[...].astype(F32)
    mid = frames[...].astype(F32) + 0.5 * total
    mid_out[...] = mid
    normed_out[...] = (normalise(mid)[0] * gain[...].reshape(1, -1)).astype(BF)
    wait_copies(copies)


def collect_kernel(ids, me_ref, scaled, near, far, out, grad_context, sems):
    wait_copies(collect(me_ref, [near, far], ids, 0, out, sems))
    inner = grad_context.shape[1]
    grad_context[...] = dot(scaled[...], out[:, 3 * inner :], 1, 0).astype(BF)


def attention_kernel(parts, window, *refs):
    place_ref, bias = refs[:2]
    segments, spans = refs[2:4]
    normed_parts = refs[4 : 4 + parts]
    grad_context, weights = refs[4 + parts : 6 + parts]
    rest = refs[6 + parts :]
    normed, context, slopes = rest[:3]
    outs = rest[3 : 3 + parts]
    halves = 1 if parts == 1 else 2
    attn_outs = rest[3 + parts : 3 + parts + halves]
    qkv, key_total, value_total, total = rest[3 + parts + halves :]
    heads = bias.shape[0]
    frames = normed.shape[0]
    own = normed_parts[0].shape[0]
    inner = context.shape[1]
    width = inner // heads
    scale = width ** (-0.5)
    firsts = places(place_ref, parts, own)
    for first, piece in zip(firsts, normed_parts):
        normed[pl.ds(first, own), :] = piece[...]
    qkv[...] = dot(normed[...], weights[:, : 3 * inner], 1, 0).astype(BF)
    seg_k, span_k = segments[...], spans[...]
    seg_q = jnp.transpose(jnp.broadcast_to(seg_k, (8, frames)))[:, :1]
    span_q = jnp.transpose(jnp.broadcast_to(span_k, (8, frames)))[:, :1]
    block = min(frames, 256)
    reach = min(window, (frames - 1) // SPAN)
    for head in range(heads):
        cols = slice(head * width, (head + 1) * width)
        key_cols = slice(inner + head * width, inner + (head + 1) * width)
        value_cols = slice(2 * inner + head * width, 2 * inner + (head + 1) * width)
        key = qkv[:, key_cols]
        value = qkv[:, value_cols]
        for first in range(0, frames, block):
            mine = slice(first, first + block)
            query = qkv[mine, cols]
            distance = span_q[mine, :] - span_k
            allowed = (seg_q[mine, :] == seg_k) & (distance >= 0) & (distance <= window)
            added = jnp.full((block, frames), bias[head, 0], F32)
            for far in range(1, reach + 1):
                added = jnp.where(distance == far, bias[head, far], added)
            scores = dot(query, key, 1, 1) * scale + added
            scores = jnp.where(allowed, scores, -1e30)
            expo = jnp.exp(scores - jnp.max(scores, axis=-1, keepdims=True))
            soft = expo / jnp.sum(expo, axis=-1, keepdims=True)
            low = soft.astype(BF)
            context[mine, cols] = dot(low, value, 1, 0).astype(BF)
            slope = grad_context[mine, cols]
            probs = dot(slope, value, 1, 1)
            probs = probs - jnp.sum(soft * probs, axis=-1, keepdims=True)
            grad = (soft * probs).astype(BF)
            slopes[mine, cols] = (dot(grad, key, 1, 0) * scale).astype(BF)
            key_slope = dot(grad, query, 0, 0)
            value_slope = dot(low, slope, 0, 0)
            if first > 0:
                key_slope = key_total[...] + key_slope
                value_slope = value_total[...] + value_slope
            if first + block < frames:
                key_total[...] = key_slope
                value_total[...] = value_slope
        slopes[:, key_cols] = (key_slope * scale).astype(BF)
        slopes[:, value_cols] = value_slope.astype(BF)
    total[...] = dot(slopes[...], weights[:, : 3 * inner], 1, 1)
    for first, out in zip(firsts, outs):
        out[...] = total[pl.ds(first, own), :].astype(BF)
    total[...] = dot(context[...], weights[:, 3 * inner :], 1, 1)
    if parts == 1:
        attn_outs[0][...] = total[...].astype(BF)
        return
    for index, out in enumerate(attn_outs):
        for at, first in enumerate((firsts[index], firsts[index + 2])):
            out[at * own : (at + 1) * own, :] = total[pl.ds(first, own), :].astype(BF)


def attention_grads_kernel(*refs):
    me_ref, normed, scaled, context, slopes = refs[:5]
    outs, total = refs[5:-1], refs[-1]
    inner = context.shape[1]
    rows = total.shape[0] // 8
    firsts = [me_ref[0] ^ mask for mask in (0, 2, 4, 6, 1, 3, 5, 7)]
    for index in range(3):
        total[...] = dot(normed[...], slopes[:, index * inner : (index + 1) * inner], 0, 0)
        hand_out(me_ref, total, firsts, rows, outs, index * inner)
    total[...] = dot(scaled[...], context[...], 0, 0)
    hand_out(me_ref, total, firsts, rows, outs, 3 * inner)


def grad_mid_kernel(parts, cot_scale, *refs):
    gain, mid, cot = refs[:3]
    pieces = refs[3 : 3 + parts]
    out = refs[3 + parts]
    upstream = pieces[0][...].astype(F32)
    for piece in pieces[1:]:
        upstream = upstream + piece[...].astype(F32)
    normed, inverse = normalise(mid[...])
    scaled = upstream * gain[...].reshape(1, -1)
    first = jnp.mean(scaled, axis=-1, keepdims=True)
    second = jnp.mean(scaled * normed, axis=-1, keepdims=True)
    slope = inverse * (scaled - first - normed * second)
    low_cot = (cot[...].astype(F32) * cot_scale).astype(BF).astype(F32)
    out[...] = (low_cot + slope).astype(BF)


def ffn_grads_kernel(parts, *refs):
    me_ref, normed, pre, hidden, down = refs[:5]
    mids = refs[5 : 5 + parts]
    outs = refs[5 + parts : -2]
    grad_mid, total = refs[-2:]
    own = mids[0].shape[0]
    rows = total.shape[0] // 8
    firsts = [me_ref[0] ^ mask for mask in (0, 2, 4, 6, 1, 3, 5, 7)]
    for index, piece in enumerate(mids):
        grad_mid[index * own : (index + 1) * own, :] = piece[...]
    total[...] = 0.5 * dot(grad_mid[...], hidden[...], 0, 0)
    hand_out(me_ref, total, firsts, rows, outs, down.shape[1])
    sigma = jax.nn.sigmoid(pre[...])
    slope = sigma * (1.0 + pre[...] * (1.0 - sigma))
    grad_hidden = (0.5 * dot(grad_mid[...], down[...], 1, 0) * slope).astype(BF)
    total[...] = dot(normed[...], grad_hidden, 0, 0)
    hand_out(me_ref, total, firsts, rows, outs, 0)


def pair_sum_kernel(keep, came, *refs):
    passed = (len(refs) - 4) // 2
    rows = keep.shape[0] // 4
    for at, out in enumerate(refs[passed : passed + 4]):
        mine = slice(at * rows, (at + 1) * rows)
        out[...] = (keep[mine, :].astype(F32) + came[mine, :].astype(F32)).astype(BF)
    for one, out in zip(refs[:passed], refs[passed + 4 :]):
        out[...] = one[...]


def half_sum_kernel(keep, came, mine, other):
    own = mine.shape[0]
    mine[...] = keep[:own, :].astype(F32) + came[:own, :].astype(F32)
    other[...] = (keep[own:, :].astype(F32) + came[own:, :].astype(F32)).astype(BF)


def row_pairs(pieces, out):
    starts = [sum(one.shape[0] for one in pieces[:at]) for at in range(len(pieces))]
    return [(one, out.at[pl.ds(at, one.shape[0]), :]) for one, at in zip(pieces, starts)]


def column_pairs(pieces, out):
    starts = [sum(one.shape[1] for one in pieces[:at]) for at in range(len(pieces))]
    return [(one, out.at[:, pl.ds(at, one.shape[1])]) for one, at in zip(pieces, starts)]


def stack_kernel(*refs):
    wait_copies(start_copies(row_pairs(refs[:-2], refs[-2]), refs[-1]))


def pack_kernel(groups, *refs):
    outs, pairs, at = refs[sum(groups) : -1], [], 0
    for count, out in zip(groups, outs):
        pairs += column_pairs(refs[at : at + count], out)
        at += count
    wait_copies(start_copies(pairs, refs[-1]))


def stack(pieces, after=()):
    total = sum(one.shape[0] for one in pieces)
    out = shape((total, pieces[0].shape[1]), BF)
    return call(stack_kernel, [out], pieces, far=len(pieces), after=after)[0]


def pack(groups, after=(), alone=False):
    outs = [
        shape((group[0].shape[0], sum(one.shape[1] for one in group)), BF) for group in groups
    ]
    whole = all(one.shape[0] % 16 == 0 and one.shape[1] % 128 == 0 for group in groups for one in group)
    if not whole:
        return [jnp.concatenate(group, axis=1) for group in groups]
    pieces = [one for group in groups for one in group]
    body = functools.partial(pack_kernel, tuple(len(group) for group in groups))
    return call(body, outs, pieces, far=len(pieces), after=after, alone=alone)


def per_device(
    frames_in,
    segment_ids,
    span_ids,
    ffn_gain,
    w_up,
    w_down,
    attn_gain,
    w_query,
    w_key,
    w_value,
    w_out,
    offset_bias,
    cotangent,
):
    dp, ctx = lax.axis_size("dp"), lax.axis_size("ctx")
    own, model = frames_in.shape[1:]
    frames = own * ctx
    heads = offset_bias.shape[0]
    window = offset_bias.shape[1] - 1
    hidden, inner = w_up.shape[1], w_query.shape[1]
    rows = w_up.shape[0]
    direct_rows = dp == 8 and rows % 16 == 0
    direct_frames = ctx == 4 and own % 16 == 0
    ids = (0, 6, 4, 2, 1, 7, 5, 3) if direct_rows else (0,)
    parts = ctx if direct_frames else 1
    part_rows = frames // parts
    me = lax.axis_index("dp").astype(jnp.int32).reshape(1)
    place = lax.axis_index("ctx").astype(jnp.int32).reshape(1)
    cot_scale = 1.0 / math.sqrt(dp * frames)

    def gather_frames(values, relay=False):
        if not direct_frames:
            return [lax.all_gather(values, "ctx", axis=0, tiled=True)]
        if relay:
            second, first = exchange(values, "ctx", 2), exchange(values, "ctx", 1)
            return [values, first, second, exchange(second, "ctx", 1)]
        return [values] + [exchange(values, "ctx", mask) for mask in (3, 2, 1)][::-1]

    def scatter_frames(pieces):
        if not direct_frames:
            return [lax.psum_scatter(pieces[0], "ctx", scatter_dimension=0, tiled=True)]
        return [pieces[0]] + [exchange(pieces[mask], "ctx", mask) for mask in (3, 2, 1)][::-1]

    def scatter_rows(pieces, passed=(), after=()):
        if not direct_rows:
            made = lax.psum_scatter(pieces[0], "dp", scatter_dimension=0, tiled=True)
            return [made], passed
        keep, send = pieces
        came = exchange(send, "dp", 1)
        outs = [shape((rows, keep.shape[1]), BF)] * 4 + [shape(one.shape, BF) for one in passed]
        sums = call(pair_sum_kernel, outs, [keep, came, *passed], after=after)
        terms = [sums[0]] + [exchange(sums[at], "dp", 2 * at) for at in (1, 2, 3)]
        return terms, sums[4:] if passed else sums[:1]

    def add_terms(terms):
        total = terms[0].astype(F32)
        for one in terms[1:]:
            total = total + one.astype(F32)
        return total

    frames_own, cot_own = frames_in[0], cotangent[0]
    both_own, ffn_rows = pack([[frames_own, cot_own], [w_up, w_down]], alone=True)
    both_parts = gather_frames(both_own, True)

    def gather_near(weight):
        return [weight] + [exchange(weight, "dp", mask) for mask in (6, 4, 2)]

    if direct_rows:
        ffn_near = stack(gather_near(ffn_rows), both_parts[1:])
        ffn_weights = [ffn_near, exchange(ffn_near, "dp", 1)]
        attn_pieces = gather_near(pack([[w_query, w_key, w_value, w_out]], [ffn_near])[0])
    else:
        ffn_weights = [lax.all_gather(ffn_rows, "dp", axis=0, tiled=True)]
        attn_weights = pack([[w_query, w_key, w_value, w_out]])[0]
        attn_weights = lax.all_gather(attn_weights, "dp", axis=0, tiled=True)
        attn_pieces = []

    ffn_normed, scaled_cot = call(
        functools.partial(prepare_kernel, parts, cot_scale),
        [shape((frames, model), BF)] * 2,
        [place, ffn_gain] + both_parts,
        smem=1,
    )
    ffn_pre, ffn_hidden, down_full, *ffn_partials = call(
        functools.partial(ffn_kernel, parts, ids),
        [shape((frames, hidden), F32), shape((frames, hidden), BF), shape((model, hidden), BF)]
        + [shape((part_rows, model), BF)] * parts,
        [me, ffn_normed] + ffn_weights,
        [pltpu.VMEM((model, hidden), BF)],
        flops=4 * frames * model * hidden,
        smem=1,
        far=2 if direct_rows else 0,
    )
    summed = scatter_frames(ffn_partials)
    near = [shape((model // 2, 4 * inner), BF)] if direct_rows else []
    mid_own, normed_own, *near = call(
        functools.partial(mid_kernel, len(summed)),
        [shape((own, model), F32), shape((own, model), BF)] + near,
        [attn_gain, frames_own] + summed + attn_pieces,
        far=len(attn_pieces),
    )
    normed_parts = gather_frames(normed_own)
    if direct_rows:
        attn_weights, grad_context = call(
            functools.partial(collect_kernel, ids),
            [shape((model, 4 * inner), BF), shape((frames, inner), BF)],
            [me, scaled_cot, near[0], exchange(near[0], "dp", 1)],
            flops=2 * frames * model * inner,
            smem=1,
            far=2,
        )
    else:
        grad_context = jnp.dot(
            scaled_cot, attn_weights[:, 3 * inner :], preferred_element_type=F32
        ).astype(BF)
    made = call(
        functools.partial(attention_kernel, parts, window),
        [
            shape((frames, model), BF),
            shape((frames, inner), BF),
            shape((frames, 3 * inner), BF),
        ]
        + [shape((part_rows, model), BF)] * parts
        + [shape((frames // 2, model), BF)] * 2 * (parts > 1)
        + [shape((frames, model), BF)] * (parts == 1),
        [place, offset_bias, segment_ids, span_ids, *normed_parts, grad_context, attn_weights],
        [
            pltpu.VMEM((frames, 3 * inner), BF),
            pltpu.VMEM((frames, inner // heads), F32),
            pltpu.VMEM((frames, inner // heads), F32),
            pltpu.VMEM((frames, model), F32),
        ],
        flops=16 * frames * model * inner + 12 * frames * frames * inner,
        smem=2,
    )
    attn_normed, context, slopes = made[:3]
    attn_partials = made[3 + parts :]
    upstream = scatter_frames(list(made[3 : 3 + parts]))
    half = [shape((model // 2, 4 * inner), BF)] * 2
    attn_grads = call(
        attention_grads_kernel,
        half if direct_rows else [shape((model, 4 * inner), BF)],
        [me, attn_normed, scaled_cot, context, slopes],
        [pltpu.VMEM((model, inner), F32)],
        flops=8 * frames * model * inner,
        smem=1,
    )
    attn_terms, attn_sums = scatter_rows(attn_grads, after=upstream[1:])
    (grad_mid_own,) = call(
        functools.partial(grad_mid_kernel, len(upstream), cot_scale),
        [shape((own, model), BF)],
        [attn_gain, mid_own, cot_own] + upstream,
    )
    grad_mid_parts = gather_frames(grad_mid_own)
    half = [shape((model // 2, 2 * hidden), BF)] * 2
    ffn_grads = call(
        functools.partial(ffn_grads_kernel, parts),
        half if direct_rows else [shape((model, 2 * hidden), BF)],
        [me, ffn_normed, ffn_pre, ffn_hidden, down_full] + grad_mid_parts,
        [pltpu.VMEM((frames, model), BF), pltpu.VMEM((model, hidden), F32)],
        flops=6 * frames * model * hidden,
        smem=1,
        after=attn_terms[1:3],
    )
    ffn_terms, passed = scatter_rows(ffn_grads, list(attn_partials[1:]))
    if direct_frames:
        keep, send = attn_partials[0], passed[0]
        attn_own, attn_far = call(
            half_sum_kernel,
            [shape((own, model), F32), shape((own, model), BF)],
            [keep, exchange(send, "ctx", 1)],
        )
        attn_sum = attn_own + exchange(attn_far, "ctx", 2).astype(F32)
    else:
        attn_sum = lax.psum_scatter(attn_partials[0], "ctx", scatter_dimension=0, tiled=True)
    block_out = (mid_own + attn_sum).astype(BF)[None]
    attn_total, ffn_total = add_terms(attn_terms), add_terms(ffn_terms)
    return (
        block_out,
        ffn_total[:, :hidden],
        ffn_total[:, hidden:],
        attn_total[:, :inner],
        attn_total[:, inner : 2 * inner],
        attn_total[:, 2 * inner : 3 * inner],
        attn_total[:, 3 * inner :],
    )


def solution(mesh):
    placed = (
        P("dp", "ctx", None),
        P("dp", None),
        P("dp", None),
        P(),
        P("dp", "ctx"),
        P("dp", "ctx"),
        P(),
        P("dp", "ctx"),
        P("dp", "ctx"),
        P("dp", "ctx"),
        P("dp", "ctx"),
        P("ctx", None),
        P("dp", "ctx", None),
    )
    return jax.shard_map(
        per_device,
        mesh=mesh,
        in_specs=placed,
        out_specs=(P("dp", "ctx", None),) + (P("dp", "ctx"),) * 6,
        check_vma=False,
    )
```

```python
import functools
import math

import jax
import jax.numpy as jnp
from jax import lax
from jax.experimental import pallas as pl
from jax.experimental.pallas import tpu as pltpu
from jax.sharding import PartitionSpec as P

SPAN = 64
BF = jnp.bfloat16
F32 = jnp.float32
MIB = 1024 * 1024


def exchange(values, axis, mask):
    size = lax.axis_size(axis)
    return lax.ppermute(values, axis, [(one, one ^ mask) for one in range(size)])


def call(body, outs, args, scratch=(), flops=0, smem=0, far=0, after=(), alone=False):
    count = len(args)
    specs = [pl.BlockSpec(memory_space=pltpu.SMEM)] * smem
    specs += [pl.BlockSpec(memory_space=pltpu.VMEM)] * (count - smem - far)
    specs += [pl.BlockSpec(memory_space=pl.ANY)] * (far + len(after))
    moved = sum(math.prod(one.shape) * one.dtype.itemsize for one in list(args) + list(outs))
    held = moved + sum(math.prod(one.shape) * jnp.dtype(one.dtype).itemsize for one in scratch)
    if far:
        scratch = [*scratch, pltpu.SemaphoreType.DMA((16,))]
    return pl.pallas_call(
        lambda *refs: body(*refs[:count], *refs[count + len(after) :]),
        out_shape=tuple(outs),
        in_specs=specs,
        out_specs=tuple(pl.BlockSpec(memory_space=pltpu.VMEM) for _ in outs),
        scratch_shapes=list(scratch),
        compiler_params=pltpu.CompilerParams(vmem_limit_bytes=60 * MIB if alone else min(held + 6 * MIB, 56 * MIB)),
        cost_estimate=pl.CostEstimate(flops=flops, bytes_accessed=moved, transcendentals=0),
    )(*args, *after)


def shape(dims, dtype):
    return jax.ShapeDtypeStruct(dims, dtype)


def dot(left, right, left_dim, right_dim):
    return lax.dot_general(
        left, right, (((left_dim,), (right_dim,)), ((), ())), preferred_element_type=F32
    )


def normalise(values):
    center = values - jnp.mean(values, axis=-1, keepdims=True)
    variance = jnp.mean(center * center, axis=-1, keepdims=True)
    inverse = lax.rsqrt(variance + 1e-05)
    return center * inverse, inverse


def start_copies(pairs, sems, first_sem=0):
    copies = []
    for at, (source, target) in enumerate(pairs):
        copies.append(pltpu.make_async_copy(source, target, sems.at[first_sem + at]))
        copies[-1].start()
    return copies


def wait_copies(copies):
    for one in copies:
        one.wait()


def collect(me_ref, pieces, ids, first_column, target, sems, first_sem=0):
    rows, width = target.shape
    rows = rows // len(ids)
    columns = slice(first_column, first_column + width)
    if len(ids) == 1:
        target[...] = pieces[0][:, columns]
        return []
    blocks = [(piece, at) for piece in pieces for at in range(0, piece.shape[0], rows)]
    pairs = []
    for (piece, at), mask in zip(blocks, ids):
        first = pl.multiple_of((me_ref[0] ^ mask) * rows, 16)
        source = piece.at[pl.ds(at, rows), pl.ds(first_column, width)]
        pairs.append((source, target.at[pl.ds(first, rows), :]))
    return start_copies(pairs, sems, first_sem)


def hand_out(me_ref, total, firsts, rows, outs, first_column):
    width = total.shape[1]
    columns = slice(first_column, first_column + width)
    if len(outs) == 1:
        outs[0][:, columns] = total[...].astype(BF)
        return
    blocks = [(out, at) for out in outs for at in range(0, out.shape[0], rows)]
    for (out, at), first in zip(blocks, firsts):
        block = total[pl.ds(pl.multiple_of(first * rows, 8), rows), :]
        out[at : at + rows, columns] = block.astype(BF)


def prepare_kernel(parts, cot_scale, *refs):
    place_ref, gain = refs[:2]
    both_parts = refs[2 : 2 + parts]
    normed_out, scaled = refs[2 + parts :]
    own, model = both_parts[0].shape[0], normed_out.shape[1]
    for index, (first, both) in enumerate(zip(places(place_ref, parts, own), both_parts)):
        normed = normalise(both[:, :model].astype(F32))[0] * gain[...].reshape(1, -1)
        normed_out[index * own : (index + 1) * own, :] = normed.astype(BF)
        cot = both[:, model:].astype(F32)
        scaled[pl.ds(first, own), :] = (cot * cot_scale).astype(BF)


def ffn_kernel(parts, ids, *refs):
    me_ref, normed = refs[:2]
    at = 3 if len(ids) == 1 else 4
    weights, rest = refs[2:at], refs[at:]
    pre_out, hidden_out, down = rest[:3]
    partials = rest[3 : 3 + parts]
    up, sems = rest[3 + parts], rest[-1]
    width = up.shape[1]
    up_copies = collect(me_ref, weights, ids, 0, up, sems)
    down_copies = collect(me_ref, weights, ids, width, down, sems, 8)
    own = partials[0].shape[0]
    wait_copies(up_copies)
    pre = dot(normed[...], up[...], 1, 0)
    pre_out[...] = pre
    hidden_out[...] = (pre * jax.nn.sigmoid(pre)).astype(BF)
    wait_copies(down_copies)
    made = dot(hidden_out[...], down[...], 1, 1)
    for index, out in enumerate(partials):
        out[...] = made[index * own : (index + 1) * own].astype(BF)


def places(place_ref, parts, own):
    if parts == 1:
        return [0]
    return [pl.multiple_of((place_ref[0] ^ mask) * own, 16) for mask in range(parts)]


def mid_kernel(parts, *refs):
    gain, frames = refs[:2]
    pieces = refs[2 : 2 + parts]
    mid_out, normed_out = refs[2 + parts :]
    total = pieces[0][...].astype(F32)
    for piece in pieces[1:]:
        total = total + piece[...].astype(F32)
    mid = frames[...].astype(F32) + 0.5 * total
    mid_out[...] = mid
    normed_out[...] = (normalise(mid)[0] * gain[...].reshape(1, -1)).astype(BF)


def collect_kernel(ids, me_ref, scaled, near, far, out, grad_context, sems):
    wait_copies(collect(me_ref, [near, far], ids, 0, out, sems))
    inner = grad_context.shape[1]
    grad_context[...] = dot(scaled[...], out[:, 3 * inner :], 1, 0).astype(BF)


def attention_kernel(parts, window, *refs):
    place_ref, bias = refs[:2]
    segments, spans = refs[2:4]
    normed_parts = refs[4 : 4 + parts]
    grad_context, weights = refs[4 + parts : 6 + parts]
    rest = refs[6 + parts :]
    normed, context, slopes = rest[:3]
    outs = rest[3 : 3 + parts]
    halves = 1 if parts == 1 else 2
    attn_outs = rest[3 + parts : 3 + parts + halves]
    qkv, key_total, value_total, total = rest[3 + parts + halves :]
    heads = bias.shape[0]
    frames = normed.shape[0]
    own = normed_parts[0].shape[0]
    inner = context.shape[1]
    width = inner // heads
    scale = width ** (-0.5)
    firsts = places(place_ref, parts, own)
    for first, piece in zip(firsts, normed_parts):
        normed[pl.ds(first, own), :] = piece[...]
    qkv[...] = dot(normed[...], weights[:, : 3 * inner], 1, 0).astype(BF)
    seg_k, span_k = segments[...], spans[...]
    seg_q = jnp.transpose(jnp.broadcast_to(seg_k, (8, frames)))[:, :1]
    span_q = jnp.transpose(jnp.broadcast_to(span_k, (8, frames)))[:, :1]
    block = min(frames, 256)
    reach = min(window, (frames - 1) // SPAN)
    for head in range(heads):
        cols = slice(head * width, (head + 1) * width)
        key_cols = slice(inner + head * width, inner + (head + 1) * width)
        value_cols = slice(2 * inner + head * width, 2 * inner + (head + 1) * width)
        key = qkv[:, key_cols]
        value = qkv[:, value_cols]
        for first in range(0, frames, block):
            mine = slice(first, first + block)
            query = qkv[mine, cols]
            distance = span_q[mine, :] - span_k
            allowed = (seg_q[mine, :] == seg_k) & (distance >= 0) & (distance <= window)
            added = jnp.full((block, frames), bias[head, 0], F32)
            for far in range(1, reach + 1):
                added = jnp.where(distance == far, bias[head, far], added)
            scores = dot(query, key, 1, 1) * scale + added
            scores = jnp.where(allowed, scores, -1e30)
            expo = jnp.exp(scores - jnp.max(scores, axis=-1, keepdims=True))
            soft = expo / jnp.sum(expo, axis=-1, keepdims=True)
            low = soft.astype(BF)
            context[mine, cols] = dot(low, value, 1, 0).astype(BF)
            slope = grad_context[mine, cols]
            probs = dot(slope, value, 1, 1)
            probs = probs - jnp.sum(soft * probs, axis=-1, keepdims=True)
            grad = (soft * probs).astype(BF)
            slopes[mine, cols] = (dot(grad, key, 1, 0) * scale).astype(BF)
            key_slope = dot(grad, query, 0, 0)
            value_slope = dot(low, slope, 0, 0)
            if first > 0:
                key_slope = key_total[...] + key_slope
                value_slope = value_total[...] + value_slope
            if first + block < frames:
                key_total[...] = key_slope
                value_total[...] = value_slope
        slopes[:, key_cols] = (key_slope * scale).astype(BF)
        slopes[:, value_cols] = value_slope.astype(BF)
    total[...] = dot(slopes[...], weights[:, : 3 * inner], 1, 1)
    for first, out in zip(firsts, outs):
        out[...] = total[pl.ds(first, own), :].astype(BF)
    total[...] = dot(context[...], weights[:, 3 * inner :], 1, 1)
    if parts == 1:
        attn_outs[0][...] = total[...].astype(BF)
        return
    for index, out in enumerate(attn_outs):
        for at, first in enumerate((firsts[index], firsts[index + 2])):
            out[at * own : (at + 1) * own, :] = total[pl.ds(first, own), :].astype(BF)


def attention_grads_kernel(*refs):
    me_ref, normed, scaled, context, slopes = refs[:5]
    outs, total = refs[5:-1], refs[-1]
    inner = context.shape[1]
    rows = total.shape[0] // 8
    firsts = [me_ref[0] ^ mask for mask in (0, 2, 4, 6, 1, 3, 5, 7)]
    for index in range(3):
        total[...] = dot(normed[...], slopes[:, index * inner : (index + 1) * inner], 0, 0)
        hand_out(me_ref, total, firsts, rows, outs, index * inner)
    total[...] = dot(scaled[...], context[...], 0, 0)
    hand_out(me_ref, total, firsts, rows, outs, 3 * inner)


def grad_mid_kernel(parts, cot_scale, *refs):
    gain, mid, cot = refs[:3]
    pieces = refs[3 : 3 + parts]
    out = refs[3 + parts]
    upstream = pieces[0][...].astype(F32)
    for piece in pieces[1:]:
        upstream = upstream + piece[...].astype(F32)
    normed, inverse = normalise(mid[...])
    scaled = upstream * gain[...].reshape(1, -1)
    first = jnp.mean(scaled, axis=-1, keepdims=True)
    second = jnp.mean(scaled * normed, axis=-1, keepdims=True)
    slope = inverse * (scaled - first - normed * second)
    low_cot = (cot[...].astype(F32) * cot_scale).astype(BF).astype(F32)
    out[...] = (low_cot + slope).astype(BF)


def ffn_grads_kernel(parts, *refs):
    me_ref, normed, pre, hidden, down = refs[:5]
    mids = refs[5 : 5 + parts]
    outs = refs[5 + parts : -2]
    grad_mid, total = refs[-2:]
    own = mids[0].shape[0]
    rows = total.shape[0] // 8
    firsts = [me_ref[0] ^ mask for mask in (0, 2, 4, 6, 1, 3, 5, 7)]
    for index, piece in enumerate(mids):
        grad_mid[index * own : (index + 1) * own, :] = piece[...]
    total[...] = 0.5 * dot(grad_mid[...], hidden[...], 0, 0)
    hand_out(me_ref, total, firsts, rows, outs, down.shape[1])
    sigma = jax.nn.sigmoid(pre[...])
    slope = sigma * (1.0 + pre[...] * (1.0 - sigma))
    grad_hidden = (0.5 * dot(grad_mid[...], down[...], 1, 0) * slope).astype(BF)
    total[...] = dot(normed[...], grad_hidden, 0, 0)
    hand_out(me_ref, total, firsts, rows, outs, 0)


def pair_sum_kernel(keep, came, *refs):
    passed = (len(refs) - 4) // 2
    rows = keep.shape[0] // 4
    for at, out in enumerate(refs[passed : passed + 4]):
        mine = slice(at * rows, (at + 1) * rows)
        out[...] = (keep[mine, :].astype(F32) + came[mine, :].astype(F32)).astype(BF)
    for one, out in zip(refs[:passed], refs[passed + 4 :]):
        out[...] = one[...]


def half_sum_kernel(keep, came, mine, other):
    own = mine.shape[0]
    mine[...] = keep[:own, :].astype(F32) + came[:own, :].astype(F32)
    other[...] = (keep[own:, :].astype(F32) + came[own:, :].astype(F32)).astype(BF)


def row_pairs(pieces, out):
    starts = [sum(one.shape[0] for one in pieces[:at]) for at in range(len(pieces))]
    return [(one, out.at[pl.ds(at, one.shape[0]), :]) for one, at in zip(pieces, starts)]


def column_pairs(pieces, out):
    starts = [sum(one.shape[1] for one in pieces[:at]) for at in range(len(pieces))]
    return [(one, out.at[:, pl.ds(at, one.shape[1])]) for one, at in zip(pieces, starts)]


def stack_kernel(*refs):
    wait_copies(start_copies(row_pairs(refs[:-2], refs[-2]), refs[-1]))


def pack_kernel(groups, *refs):
    outs, pairs, at = refs[sum(groups) : -1], [], 0
    for count, out in zip(groups, outs):
        pairs += column_pairs(refs[at : at + count], out)
        at += count
    wait_copies(start_copies(pairs, refs[-1]))


def stack(pieces, after=()):
    total = sum(one.shape[0] for one in pieces)
    out = shape((total, pieces[0].shape[1]), BF)
    return call(stack_kernel, [out], pieces, far=len(pieces), after=after)[0]


def pack(groups, after=(), alone=False):
    outs = [
        shape((group[0].shape[0], sum(one.shape[1] for one in group)), BF) for group in groups
    ]
    whole = all(one.shape[0] % 16 == 0 and one.shape[1] % 128 == 0 for group in groups for one in group)
    if not whole:
        return [jnp.concatenate(group, axis=1) for group in groups]
    pieces = [one for group in groups for one in group]
    body = functools.partial(pack_kernel, tuple(len(group) for group in groups))
    return call(body, outs, pieces, far=len(pieces), after=after, alone=alone)


def per_device(
    frames_in,
    segment_ids,
    span_ids,
    ffn_gain,
    w_up,
    w_down,
    attn_gain,
    w_query,
    w_key,
    w_value,
    w_out,
    offset_bias,
    cotangent,
):
    dp, ctx = lax.axis_size("dp"), lax.axis_size("ctx")
    own, model = frames_in.shape[1:]
    frames = own * ctx
    heads = offset_bias.shape[0]
    window = offset_bias.shape[1] - 1
    hidden, inner = w_up.shape[1], w_query.shape[1]
    rows = w_up.shape[0]
    direct_rows = dp == 8 and rows % 16 == 0
    direct_frames = ctx == 4 and own % 16 == 0
    ids = (0, 6, 4, 2, 1, 7, 5, 3) if direct_rows else (0,)
    parts = ctx if direct_frames else 1
    part_rows = frames // parts
    me = lax.axis_index("dp").astype(jnp.int32).reshape(1)
    place = lax.axis_index("ctx").astype(jnp.int32).reshape(1)
    cot_scale = 1.0 / math.sqrt(dp * frames)

    def gather_frames(values, relay=False):
        if not direct_frames:
            return [lax.all_gather(values, "ctx", axis=0, tiled=True)]
        if relay:
            second, first = exchange(values, "ctx", 2), exchange(values, "ctx", 1)
            return [values, first, second, exchange(second, "ctx", 1)]
        return [values] + [exchange(values, "ctx", mask) for mask in (3, 2, 1)][::-1]

    def scatter_frames(pieces):
        if not direct_frames:
            return [lax.psum_scatter(pieces[0], "ctx", scatter_dimension=0, tiled=True)]
        return [pieces[0]] + [exchange(pieces[mask], "ctx", mask) for mask in (3, 2, 1)][::-1]

    def scatter_rows(pieces, passed=(), after=()):
        if not direct_rows:
            made = lax.psum_scatter(pieces[0], "dp", scatter_dimension=0, tiled=True)
            return [made], passed
        keep, send = pieces
        came = exchange(send, "dp", 1)
        outs = [shape((rows, keep.shape[1]), BF)] * 4 + [shape(one.shape, BF) for one in passed]
        sums = call(pair_sum_kernel, outs, [keep, came, *passed], after=after)
        terms = [sums[0]] + [exchange(sums[at], "dp", 2 * at) for at in (1, 2, 3)]
        return terms, sums[4:] if passed else sums[:1]

    def add_terms(terms):
        total = terms[0].astype(F32)
        for one in terms[1:]:
            total = total + one.astype(F32)
        return total

    frames_own, cot_own = frames_in[0], cotangent[0]
    both_own, ffn_rows = pack([[frames_own, cot_own], [w_up, w_down]], alone=True)
    both_parts = gather_frames(both_own, True)

    def gather_near(weight):
        return [weight] + [exchange(weight, "dp", mask) for mask in (6, 4, 2)]

    if direct_rows:
        ffn_near = stack(gather_near(ffn_rows), both_parts[1:])
        ffn_weights = [ffn_near, exchange(ffn_near, "dp", 1)]
        attn_pieces = gather_near(pack([[w_query, w_key, w_value, w_out]], [ffn_near])[0])
    else:
        ffn_weights = [lax.all_gather(ffn_rows, "dp", axis=0, tiled=True)]
        attn_weights = pack([[w_query, w_key, w_value, w_out]])[0]
        attn_weights = lax.all_gather(attn_weights, "dp", axis=0, tiled=True)
        attn_pieces = []

    ffn_normed, scaled_cot = call(
        functools.partial(prepare_kernel, parts, cot_scale),
        [shape((frames, model), BF)] * 2,
        [place, ffn_gain] + both_parts,
        smem=1,
    )
    ffn_pre, ffn_hidden, down_full, *ffn_partials = call(
        functools.partial(ffn_kernel, parts, ids),
        [shape((frames, hidden), F32), shape((frames, hidden), BF), shape((model, hidden), BF)]
        + [shape((part_rows, model), BF)] * parts,
        [me, ffn_normed] + ffn_weights,
        [pltpu.VMEM((model, hidden), BF)],
        flops=4 * frames * model * hidden,
        smem=1,
        far=2 if direct_rows else 0,
    )
    summed = scatter_frames(ffn_partials)
    mid_own, normed_own = call(
        functools.partial(mid_kernel, len(summed)),
        [shape((own, model), F32), shape((own, model), BF)],
        [attn_gain, frames_own] + summed,
        after=attn_pieces[1:],
    )
    normed_parts = gather_frames(normed_own)
    if direct_rows:
        near = stack(attn_pieces, [normed_own])
        attn_weights, grad_context = call(
            functools.partial(collect_kernel, ids),
            [shape((model, 4 * inner), BF), shape((frames, inner), BF)],
            [me, scaled_cot, near, exchange(near, "dp", 1)],
            flops=2 * frames * model * inner,
            smem=1,
            far=2,
        )
    else:
        grad_context = jnp.dot(
            scaled_cot, attn_weights[:, 3 * inner :], preferred_element_type=F32
        ).astype(BF)
    made = call(
        functools.partial(attention_kernel, parts, window),
        [
            shape((frames, model), BF),
            shape((frames, inner), BF),
            shape((frames, 3 * inner), BF),
        ]
        + [shape((part_rows, model), BF)] * parts
        + [shape((frames // 2, model), BF)] * 2 * (parts > 1)
        + [shape((frames, model), BF)] * (parts == 1),
        [place, offset_bias, segment_ids, span_ids, *normed_parts, grad_context, attn_weights],
        [
            pltpu.VMEM((frames, 3 * inner), BF),
            pltpu.VMEM((frames, inner // heads), F32),
            pltpu.VMEM((frames, inner // heads), F32),
            pltpu.VMEM((frames, model), F32),
        ],
        flops=16 * frames * model * inner + 12 * frames * frames * inner,
        smem=2,
    )
    attn_normed, context, slopes = made[:3]
    attn_partials = made[3 + parts :]
    upstream = scatter_frames(list(made[3 : 3 + parts]))
    half = [shape((model // 2, 4 * inner), BF)] * 2
    attn_grads = call(
        attention_grads_kernel,
        half if direct_rows else [shape((model, 4 * inner), BF)],
        [me, attn_normed, scaled_cot, context, slopes],
        [pltpu.VMEM((model, inner), F32)],
        flops=8 * frames * model * inner,
        smem=1,
    )
    attn_terms, attn_sums = scatter_rows(attn_grads, after=upstream[1:])
    (grad_mid_own,) = call(
        functools.partial(grad_mid_kernel, len(upstream), cot_scale),
        [shape((own, model), BF)],
        [attn_gain, mid_own, cot_own] + upstream,
    )
    grad_mid_parts = gather_frames(grad_mid_own)
    half = [shape((model // 2, 2 * hidden), BF)] * 2
    ffn_grads = call(
        functools.partial(ffn_grads_kernel, parts),
        half if direct_rows else [shape((model, 2 * hidden), BF)],
        [me, ffn_normed, ffn_pre, ffn_hidden, down_full] + grad_mid_parts,
        [pltpu.VMEM((frames, model), BF), pltpu.VMEM((model, hidden), F32)],
        flops=6 * frames * model * hidden,
        smem=1,
        after=attn_terms[1:3],
    )
    ffn_terms, passed = scatter_rows(ffn_grads, list(attn_partials[1:]))
    if direct_frames:
        keep, send = attn_partials[0], passed[0]
        attn_own, attn_far = call(
            half_sum_kernel,
            [shape((own, model), F32), shape((own, model), BF)],
            [keep, exchange(send, "ctx", 1)],
        )
        attn_sum = attn_own + exchange(attn_far, "ctx", 2).astype(F32)
    else:
        attn_sum = lax.psum_scatter(attn_partials[0], "ctx", scatter_dimension=0, tiled=True)
    block_out = (mid_own + attn_sum).astype(BF)[None]
    attn_total, ffn_total = add_terms(attn_terms), add_terms(ffn_terms)
    return (
        block_out,
        ffn_total[:, :hidden],
        ffn_total[:, hidden:],
        attn_total[:, :inner],
        attn_total[:, inner : 2 * inner],
        attn_total[:, 2 * inner : 3 * inner],
        attn_total[:, 3 * inner :],
    )


def solution(mesh):
    placed = (
        P("dp", "ctx", None),
        P("dp", None),
        P("dp", None),
        P(),
        P("dp", "ctx"),
        P("dp", "ctx"),
        P(),
        P("dp", "ctx"),
        P("dp", "ctx"),
        P("dp", "ctx"),
        P("dp", "ctx"),
        P("ctx", None),
        P("dp", "ctx", None),
    )
    return jax.shard_map(
        per_device,
        mesh=mesh,
        in_specs=placed,
        out_specs=(P("dp", "ctx", None),) + (P("dp", "ctx"),) * 6,
        check_vma=False,
    )
```

```python
import functools
import math

import jax
import jax.numpy as jnp
from jax import lax
from jax.experimental import pallas as pl
from jax.experimental.pallas import tpu as pltpu
from jax.sharding import PartitionSpec as P

SPAN = 64
BF = jnp.bfloat16
F32 = jnp.float32
MIB = 1024 * 1024


def exchange(values, axis, mask):
    size = lax.axis_size(axis)
    return lax.ppermute(values, axis, [(one, one ^ mask) for one in range(size)])


def call(body, outs, args, scratch=(), flops=0, smem=0, far=0, after=(), alone=False):
    count = len(args)
    specs = [pl.BlockSpec(memory_space=pltpu.SMEM)] * smem
    specs += [pl.BlockSpec(memory_space=pltpu.VMEM)] * (count - smem - far)
    specs += [pl.BlockSpec(memory_space=pl.ANY)] * (far + len(after))
    moved = sum(math.prod(one.shape) * one.dtype.itemsize for one in list(args) + list(outs))
    held = moved + sum(math.prod(one.shape) * jnp.dtype(one.dtype).itemsize for one in scratch)
    if far:
        scratch = [*scratch, pltpu.SemaphoreType.DMA((16,))]
    return pl.pallas_call(
        lambda *refs: body(*refs[:count], *refs[count + len(after) :]),
        out_shape=tuple(outs),
        in_specs=specs,
        out_specs=tuple(pl.BlockSpec(memory_space=pltpu.VMEM) for _ in outs),
        scratch_shapes=list(scratch),
        compiler_params=pltpu.CompilerParams(vmem_limit_bytes=60 * MIB if alone else min(held + 6 * MIB, 56 * MIB)),
        cost_estimate=pl.CostEstimate(flops=flops, bytes_accessed=moved, transcendentals=0),
    )(*args, *after)


def shape(dims, dtype):
    return jax.ShapeDtypeStruct(dims, dtype)


def dot(left, right, left_dim, right_dim):
    return lax.dot_general(
        left, right, (((left_dim,), (right_dim,)), ((), ())), preferred_element_type=F32
    )


def normalise(values):
    center = values - jnp.mean(values, axis=-1, keepdims=True)
    variance = jnp.mean(center * center, axis=-1, keepdims=True)
    inverse = lax.rsqrt(variance + 1e-05)
    return center * inverse, inverse


def start_copies(pairs, sems, first_sem=0):
    copies = []
    for at, (source, target) in enumerate(pairs):
        copies.append(pltpu.make_async_copy(source, target, sems.at[first_sem + at]))
        copies[-1].start()
    return copies


def wait_copies(copies):
    for one in copies:
        one.wait()


def collect(me_ref, pieces, ids, first_column, target, sems, first_sem=0):
    rows, width = target.shape
    rows = rows // len(ids)
    columns = slice(first_column, first_column + width)
    if len(ids) == 1:
        target[...] = pieces[0][:, columns]
        return []
    blocks = [(piece, at) for piece in pieces for at in range(0, piece.shape[0], rows)]
    pairs = []
    for (piece, at), mask in zip(blocks, ids):
        first = pl.multiple_of((me_ref[0] ^ mask) * rows, 16)
        source = piece.at[pl.ds(at, rows), pl.ds(first_column, width)]
        pairs.append((source, target.at[pl.ds(first, rows), :]))
    return start_copies(pairs, sems, first_sem)


def hand_out(me_ref, total, firsts, rows, outs, first_column):
    width = total.shape[1]
    columns = slice(first_column, first_column + width)
    if len(outs) == 1:
        outs[0][:, columns] = total[...].astype(BF)
        return
    blocks = [(out, at) for out in outs for at in range(0, out.shape[0], rows)]
    for (out, at), first in zip(blocks, firsts):
        block = total[pl.ds(pl.multiple_of(first * rows, 8), rows), :]
        out[at : at + rows, columns] = block.astype(BF)


def prepare_kernel(parts, cot_scale, *refs):
    place_ref, gain = refs[:2]
    both_parts = refs[2 : 2 + parts]
    normed_out, scaled = refs[2 + parts :]
    own, model = both_parts[0].shape[0], normed_out.shape[1]
    for index, (first, both) in enumerate(zip(places(place_ref, parts, own), both_parts)):
        normed = normalise(both[:, :model].astype(F32))[0] * gain[...].reshape(1, -1)
        normed_out[index * own : (index + 1) * own, :] = normed.astype(BF)
        cot = both[:, model:].astype(F32)
        scaled[pl.ds(first, own), :] = (cot * cot_scale).astype(BF)


def ffn_kernel(parts, ids, *refs):
    me_ref, normed = refs[:2]
    at = 3 if len(ids) == 1 else 4
    weights, rest = refs[2:at], refs[at:]
    pre_out, hidden_out, down = rest[:3]
    partials = rest[3 : 3 + parts]
    up, sems = rest[3 + parts], rest[-1]
    width = up.shape[1]
    up_copies = collect(me_ref, weights, ids, 0, up, sems)
    down_copies = collect(me_ref, weights, ids, width, down, sems, 8)
    own = partials[0].shape[0]
    wait_copies(up_copies)
    pre = dot(normed[...], up[...], 1, 0)
    pre_out[...] = pre
    hidden_out[...] = (pre * jax.nn.sigmoid(pre)).astype(BF)
    wait_copies(down_copies)
    made = dot(hidden_out[...], down[...], 1, 1)
    for index, out in enumerate(partials):
        out[...] = made[index * own : (index + 1) * own].astype(BF)


def places(place_ref, parts, own):
    if parts == 1:
        return [0]
    return [pl.multiple_of((place_ref[0] ^ mask) * own, 16) for mask in range(parts)]


def mid_kernel(parts, *refs):
    gain, frames = refs[:2]
    pieces = refs[2 : 2 + parts]
    mid_out, normed_out = refs[2 + parts :]
    total = pieces[0][...].astype(F32)
    for piece in pieces[1:]:
        total = total + piece[...].astype(F32)
    mid = frames[...].astype(F32) + 0.5 * total
    mid_out[...] = mid
    normed_out[...] = (normalise(mid)[0] * gain[...].reshape(1, -1)).astype(BF)


def collect_kernel(ids, me_ref, scaled, near, far, out, grad_context, sems):
    wait_copies(collect(me_ref, [near, far], ids, 0, out, sems))
    inner = grad_context.shape[1]
    grad_context[...] = dot(scaled[...], out[:, 3 * inner :], 1, 0).astype(BF)


def attention_kernel(parts, window, *refs):
    place_ref, bias = refs[:2]
    segments, spans = refs[2:4]
    normed_parts = refs[4 : 4 + parts]
    grad_context, weights = refs[4 + parts : 6 + parts]
    rest = refs[6 + parts :]
    normed, context, slopes = rest[:3]
    outs = rest[3 : 3 + parts]
    halves = 1 if parts == 1 else 2
    attn_outs = rest[3 + parts : 3 + parts + halves]
    qkv, key_total, value_total, total = rest[3 + parts + halves :]
    heads = bias.shape[0]
    frames = normed.shape[0]
    own = normed_parts[0].shape[0]
    inner = context.shape[1]
    width = inner // heads
    scale = width ** (-0.5)
    firsts = places(place_ref, parts, own)
    for first, piece in zip(firsts, normed_parts):
        normed[pl.ds(first, own), :] = piece[...]
    qkv[...] = dot(normed[...], weights[:, : 3 * inner], 1, 0).astype(BF)
    seg_k, span_k = segments[...], spans[...]
    seg_q = jnp.transpose(jnp.broadcast_to(seg_k, (8, frames)))[:, :1]
    span_q = jnp.transpose(jnp.broadcast_to(span_k, (8, frames)))[:, :1]
    block = min(frames, 256)
    reach = min(window, (frames - 1) // SPAN)
    starts = range(0, frames, block)
    masks = []
    for first in starts:
        mine = slice(first, first + block)
        distance = jnp.where(seg_q[mine, :] == seg_k, span_q[mine, :] - span_k, -1)
        masks.append([distance == far for far in range(reach + 1)])
    for head in range(heads):
        cols = slice(head * width, (head + 1) * width)
        key_cols = slice(inner + head * width, inner + (head + 1) * width)
        value_cols = slice(2 * inner + head * width, 2 * inner + (head + 1) * width)
        key = qkv[:, key_cols]
        value = qkv[:, value_cols]
        for first, far_masks in zip(starts, masks):
            mine = slice(first, first + block)
            query = qkv[mine, cols]
            added = jnp.full((block, frames), -1e30, F32)
            for far, mask in enumerate(far_masks):
                added = jnp.where(mask, bias[head, far], added)
            scores = dot(query, key, 1, 1) * scale + added
            expo = jnp.exp(scores - jnp.max(scores, axis=-1, keepdims=True))
            soft = expo * (1.0 / jnp.sum(expo, axis=-1, keepdims=True))
            low = soft.astype(BF)
            context[mine, cols] = dot(low, value, 1, 0).astype(BF)
            slope = grad_context[mine, cols]
            probs = dot(slope, value, 1, 1)
            probs = probs - jnp.sum(soft * probs, axis=-1, keepdims=True)
            grad = (soft * probs).astype(BF)
            slopes[mine, cols] = (dot(grad, key, 1, 0) * scale).astype(BF)
            key_slope = dot(grad, query, 0, 0)
            value_slope = dot(low, slope, 0, 0)
            if first > 0:
                key_slope = key_total[...] + key_slope
                value_slope = value_total[...] + value_slope
            if first + block < frames:
                key_total[...] = key_slope
                value_total[...] = value_slope
        slopes[:, key_cols] = (key_slope * scale).astype(BF)
        slopes[:, value_cols] = value_slope.astype(BF)
    total[...] = dot(slopes[...], weights[:, : 3 * inner], 1, 1)
    for first, out in zip(firsts, outs):
        out[...] = total[pl.ds(first, own), :].astype(BF)
    total[...] = dot(context[...], weights[:, 3 * inner :], 1, 1)
    if parts == 1:
        attn_outs[0][...] = total[...].astype(BF)
        return
    for index, out in enumerate(attn_outs):
        for at, first in enumerate((firsts[index], firsts[index + 2])):
            out[at * own : (at + 1) * own, :] = total[pl.ds(first, own), :].astype(BF)


def attention_grads_kernel(*refs):
    me_ref, normed, scaled, context, slopes = refs[:5]
    outs, total = refs[5:-1], refs[-1]
    inner = context.shape[1]
    rows = total.shape[0] // 8
    firsts = [me_ref[0] ^ mask for mask in (0, 2, 4, 6, 1, 3, 5, 7)]
    for index in range(3):
        total[...] = dot(normed[...], slopes[:, index * inner : (index + 1) * inner], 0, 0)
        hand_out(me_ref, total, firsts, rows, outs, index * inner)
    total[...] = dot(scaled[...], context[...], 0, 0)
    hand_out(me_ref, total, firsts, rows, outs, 3 * inner)


def grad_mid_kernel(parts, cot_scale, *refs):
    gain, mid, cot = refs[:3]
    pieces = refs[3 : 3 + parts]
    out = refs[3 + parts]
    upstream = pieces[0][...].astype(F32)
    for piece in pieces[1:]:
        upstream = upstream + piece[...].astype(F32)
    normed, inverse = normalise(mid[...])
    scaled = upstream * gain[...].reshape(1, -1)
    first = jnp.mean(scaled, axis=-1, keepdims=True)
    second = jnp.mean(scaled * normed, axis=-1, keepdims=True)
    slope = inverse * (scaled - first - normed * second)
    low_cot = (cot[...].astype(F32) * cot_scale).astype(BF).astype(F32)
    out[...] = (low_cot + slope).astype(BF)


def ffn_grads_kernel(parts, *refs):
    me_ref, normed, pre, hidden, down = refs[:5]
    mids = refs[5 : 5 + parts]
    outs = refs[5 + parts : -2]
    grad_mid, total = refs[-2:]
    own = mids[0].shape[0]
    rows = total.shape[0] // 8
    firsts = [me_ref[0] ^ mask for mask in (0, 2, 4, 6, 1, 3, 5, 7)]
    for index, piece in enumerate(mids):
        grad_mid[index * own : (index + 1) * own, :] = piece[...]
    total[...] = 0.5 * dot(grad_mid[...], hidden[...], 0, 0)
    hand_out(me_ref, total, firsts, rows, outs, down.shape[1])
    sigma = jax.nn.sigmoid(pre[...])
    slope = sigma * (1.0 + pre[...] * (1.0 - sigma))
    grad_hidden = (0.5 * dot(grad_mid[...], down[...], 1, 0) * slope).astype(BF)
    total[...] = dot(normed[...], grad_hidden, 0, 0)
    hand_out(me_ref, total, firsts, rows, outs, 0)


def pair_sum_kernel(keep, came, *refs):
    passed = (len(refs) - 4) // 2
    rows = keep.shape[0] // 4
    for at, out in enumerate(refs[passed : passed + 4]):
        mine = slice(at * rows, (at + 1) * rows)
        out[...] = (keep[mine, :].astype(F32) + came[mine, :].astype(F32)).astype(BF)
    for one, out in zip(refs[:passed], refs[passed + 4 :]):
        out[...] = one[...]


def half_sum_kernel(keep, came, mine, other):
    own = mine.shape[0]
    mine[...] = keep[:own, :].astype(F32) + came[:own, :].astype(F32)
    other[...] = (keep[own:, :].astype(F32) + came[own:, :].astype(F32)).astype(BF)


def row_pairs(pieces, out):
    starts = [sum(one.shape[0] for one in pieces[:at]) for at in range(len(pieces))]
    return [(one, out.at[pl.ds(at, one.shape[0]), :]) for one, at in zip(pieces, starts)]


def column_pairs(pieces, out):
    starts = [sum(one.shape[1] for one in pieces[:at]) for at in range(len(pieces))]
    return [(one, out.at[:, pl.ds(at, one.shape[1])]) for one, at in zip(pieces, starts)]


def stack_kernel(*refs):
    wait_copies(start_copies(row_pairs(refs[:-2], refs[-2]), refs[-1]))


def pack_kernel(groups, *refs):
    outs, pairs, at = refs[sum(groups) : -1], [], 0
    for count, out in zip(groups, outs):
        pairs += column_pairs(refs[at : at + count], out)
        at += count
    wait_copies(start_copies(pairs, refs[-1]))


def stack(pieces, after=()):
    total = sum(one.shape[0] for one in pieces)
    out = shape((total, pieces[0].shape[1]), BF)
    return call(stack_kernel, [out], pieces, far=len(pieces), after=after)[0]


def pack(groups, after=(), alone=False):
    outs = [
        shape((group[0].shape[0], sum(one.shape[1] for one in group)), BF) for group in groups
    ]
    whole = all(one.shape[0] % 16 == 0 and one.shape[1] % 128 == 0 for group in groups for one in group)
    if not whole:
        return [jnp.concatenate(group, axis=1) for group in groups]
    pieces = [one for group in groups for one in group]
    body = functools.partial(pack_kernel, tuple(len(group) for group in groups))
    return call(body, outs, pieces, far=len(pieces), after=after, alone=alone)


def per_device(
    frames_in,
    segment_ids,
    span_ids,
    ffn_gain,
    w_up,
    w_down,
    attn_gain,
    w_query,
    w_key,
    w_value,
    w_out,
    offset_bias,
    cotangent,
):
    dp, ctx = lax.axis_size("dp"), lax.axis_size("ctx")
    own, model = frames_in.shape[1:]
    frames = own * ctx
    heads = offset_bias.shape[0]
    window = offset_bias.shape[1] - 1
    hidden, inner = w_up.shape[1], w_query.shape[1]
    rows = w_up.shape[0]
    direct_rows = dp == 8 and rows % 16 == 0
    direct_frames = ctx == 4 and own % 16 == 0
    ids = (0, 6, 4, 2, 1, 7, 5, 3) if direct_rows else (0,)
    parts = ctx if direct_frames else 1
    part_rows = frames // parts
    me = lax.axis_index("dp").astype(jnp.int32).reshape(1)
    place = lax.axis_index("ctx").astype(jnp.int32).reshape(1)
    cot_scale = 1.0 / math.sqrt(dp * frames)

    def gather_frames(values, relay=False):
        if not direct_frames:
            return [lax.all_gather(values, "ctx", axis=0, tiled=True)]
        if relay:
            second, first = exchange(values, "ctx", 2), exchange(values, "ctx", 1)
            return [values, first, second, exchange(second, "ctx", 1)]
        return [values] + [exchange(values, "ctx", mask) for mask in (3, 2, 1)][::-1]

    def scatter_frames(pieces):
        if not direct_frames:
            return [lax.psum_scatter(pieces[0], "ctx", scatter_dimension=0, tiled=True)]
        return [pieces[0]] + [exchange(pieces[mask], "ctx", mask) for mask in (3, 2, 1)][::-1]

    def scatter_rows(pieces, passed=(), after=()):
        if not direct_rows:
            made = lax.psum_scatter(pieces[0], "dp", scatter_dimension=0, tiled=True)
            return [made], passed
        keep, send = pieces
        came = exchange(send, "dp", 1)
        outs = [shape((rows, keep.shape[1]), BF)] * 4 + [shape(one.shape, BF) for one in passed]
        sums = call(pair_sum_kernel, outs, [keep, came, *passed], after=after)
        terms = [sums[0]] + [exchange(sums[at], "dp", 2 * at) for at in (1, 2, 3)]
        return terms, sums[4:] if passed else sums[:1]

    def add_terms(terms):
        total = terms[0].astype(F32)
        for one in terms[1:]:
            total = total + one.astype(F32)
        return total

    frames_own, cot_own = frames_in[0], cotangent[0]
    both_own, ffn_rows = pack([[frames_own, cot_own], [w_up, w_down]], alone=True)
    both_parts = gather_frames(both_own, True)

    def gather_near(weight):
        return [weight] + [exchange(weight, "dp", mask) for mask in (6, 4, 2)]

    if direct_rows:
        ffn_near = stack(gather_near(ffn_rows), both_parts[1:])
        ffn_weights = [ffn_near, exchange(ffn_near, "dp", 1)]
        attn_pieces = gather_near(pack([[w_query, w_key, w_value, w_out]], [ffn_near])[0])
    else:
        ffn_weights = [lax.all_gather(ffn_rows, "dp", axis=0, tiled=True)]
        attn_weights = pack([[w_query, w_key, w_value, w_out]])[0]
        attn_weights = lax.all_gather(attn_weights, "dp", axis=0, tiled=True)
        attn_pieces = []

    ffn_normed, scaled_cot = call(
        functools.partial(prepare_kernel, parts, cot_scale),
        [shape((frames, model), BF)] * 2,
        [place, ffn_gain] + both_parts,
        smem=1,
    )
    ffn_pre, ffn_hidden, down_full, *ffn_partials = call(
        functools.partial(ffn_kernel, parts, ids),
        [shape((frames, hidden), F32), shape((frames, hidden), BF), shape((model, hidden), BF)]
        + [shape((part_rows, model), BF)] * parts,
        [me, ffn_normed] + ffn_weights,
        [pltpu.VMEM((model, hidden), BF)],
        flops=4 * frames * model * hidden,
        smem=1,
        far=2 if direct_rows else 0,
    )
    summed = scatter_frames(ffn_partials)
    mid_own, normed_own = call(
        functools.partial(mid_kernel, len(summed)),
        [shape((own, model), F32), shape((own, model), BF)],
        [attn_gain, frames_own] + summed,
        after=attn_pieces[1:],
    )
    normed_parts = gather_frames(normed_own)
    if direct_rows:
        near = stack(attn_pieces, [normed_own])
        attn_weights, grad_context = call(
            functools.partial(collect_kernel, ids),
            [shape((model, 4 * inner), BF), shape((frames, inner), BF)],
            [me, scaled_cot, near, exchange(near, "dp", 1)],
            flops=2 * frames * model * inner,
            smem=1,
            far=2,
        )
    else:
        grad_context = jnp.dot(
            scaled_cot, attn_weights[:, 3 * inner :], preferred_element_type=F32
        ).astype(BF)
    made = call(
        functools.partial(attention_kernel, parts, window),
        [
            shape((frames, model), BF),
            shape((frames, inner), BF),
            shape((frames, 3 * inner), BF),
        ]
        + [shape((part_rows, model), BF)] * parts
        + [shape((frames // 2, model), BF)] * 2 * (parts > 1)
        + [shape((frames, model), BF)] * (parts == 1),
        [place, offset_bias, segment_ids, span_ids, *normed_parts, grad_context, attn_weights],
        [
            pltpu.VMEM((frames, 3 * inner), BF),
            pltpu.VMEM((frames, inner // heads), F32),
            pltpu.VMEM((frames, inner // heads), F32),
            pltpu.VMEM((frames, model), F32),
        ],
        flops=16 * frames * model * inner + 12 * frames * frames * inner,
        smem=2,
    )
    attn_normed, context, slopes = made[:3]
    attn_partials = made[3 + parts :]
    upstream = scatter_frames(list(made[3 : 3 + parts]))
    half = [shape((model // 2, 4 * inner), BF)] * 2
    attn_grads = call(
        attention_grads_kernel,
        half if direct_rows else [shape((model, 4 * inner), BF)],
        [me, attn_normed, scaled_cot, context, slopes],
        [pltpu.VMEM((model, inner), F32)],
        flops=8 * frames * model * inner,
        smem=1,
    )
    attn_terms, attn_sums = scatter_rows(attn_grads, after=upstream[1:])
    (grad_mid_own,) = call(
        functools.partial(grad_mid_kernel, len(upstream), cot_scale),
        [shape((own, model), BF)],
        [attn_gain, mid_own, cot_own] + upstream,
    )
    grad_mid_parts = gather_frames(grad_mid_own)
    half = [shape((model // 2, 2 * hidden), BF)] * 2
    ffn_grads = call(
        functools.partial(ffn_grads_kernel, parts),
        half if direct_rows else [shape((model, 2 * hidden), BF)],
        [me, ffn_normed, ffn_pre, ffn_hidden, down_full] + grad_mid_parts,
        [pltpu.VMEM((frames, model), BF), pltpu.VMEM((model, hidden), F32)],
        flops=6 * frames * model * hidden,
        smem=1,
        after=attn_terms[1:3],
    )
    ffn_terms, passed = scatter_rows(ffn_grads, list(attn_partials[1:]))
    if direct_frames:
        keep, send = attn_partials[0], passed[0]
        attn_own, attn_far = call(
            half_sum_kernel,
            [shape((own, model), F32), shape((own, model), BF)],
            [keep, exchange(send, "ctx", 1)],
        )
        attn_sum = attn_own + exchange(attn_far, "ctx", 2).astype(F32)
    else:
        attn_sum = lax.psum_scatter(attn_partials[0], "ctx", scatter_dimension=0, tiled=True)
    block_out = (mid_own + attn_sum).astype(BF)[None]
    attn_total, ffn_total = add_terms(attn_terms), add_terms(ffn_terms)
    return (
        block_out,
        ffn_total[:, :hidden],
        ffn_total[:, hidden:],
        attn_total[:, :inner],
        attn_total[:, inner : 2 * inner],
        attn_total[:, 2 * inner : 3 * inner],
        attn_total[:, 3 * inner :],
    )


def solution(mesh):
    placed = (
        P("dp", "ctx", None),
        P("dp", None),
        P("dp", None),
        P(),
        P("dp", "ctx"),
        P("dp", "ctx"),
        P(),
        P("dp", "ctx"),
        P("dp", "ctx"),
        P("dp", "ctx"),
        P("dp", "ctx"),
        P("ctx", None),
        P("dp", "ctx", None),
    )
    return jax.shard_map(
        per_device,
        mesh=mesh,
        in_specs=placed,
        out_specs=(P("dp", "ctx", None),) + (P("dp", "ctx"),) * 6,
        check_vma=False,
    )
```
